256 devices in a mesh: dp: 64 (over z, x, core), sub: 4 (over y).
Axes of the slice: x: 4, y: 4, z: 8, core: 2. Of those that a mesh axis runs over, the one named last changes fastest.
Arguments:
- embeddings: bfloat16 [256, 512, 1024], P('dp', 'sub'), may hold values from -6 to 6
- cluster_ids: int32 [256, 512], P('dp', 'sub'), may hold values from 0 to 15
- valid: int32 [256, 512], P('dp', 'sub'), may hold values 0 or 1
- pair_left: int32 [2048], P('dp'), may hold values from 0 to 255, as said below
- pair_right: int32 [2048], P('dp'), may hold values from 0 to 255, as said below
Outputs:
- best_match: float32 [256, 512], P('dp', 'sub')
The draws below stay inside these ranges and needn't reach their ends.
Inputs may be any that keep to these rules, and one draw needn't show every extreme that they name: pair_left[p] is one of the 4 blocks of index p // 32 of dp, that is, it lies in [(p // 32) * 4, (p // 32 + 1) * 4). The 32 pairs listed for one index of dp name second blocks held by 32 different indices of dp, one pair for each of them and none for the other 32; a block is held by index pair_right // 4.
All inputs are finite; a program needn't handle non-finite values. No bound on the sum of `valid` on one device may be relied on, other than what follows from the above.
Results may differ from the reference program's by a relative error of at most 0.00037.
Values may be sent and summed in bfloat16 or wider, within the bound.
No kernel may reach another device: no remote copies, remote signals or barrier semaphores. Data moves between devices by JAX's collectives and lax.ppermute only.
A program may use at most 128 MiB of HBM per device.

```python
import math
import jax
import jax.numpy as jnp
import numpy as np
from jax import lax

DIM = 1024
BR = 512
BLK_GRP = 4
CAP = 1
CLUSTERS = 16
PAIR_GRP = 32
PAIRS = 2048
NBLK = 256


def pair_tables(key):
    groups = PAIRS // PAIR_GRP
    key_peer, key_order, key_right, key_left = jax.random.split(key, 4)
    peer_scores = jax.random.randint(key_peer, (groups, groups), 0, 1 << 20) * groups + jnp.arange(groups)[None, :]
    peers = jnp.argsort(peer_scores, axis=1).astype(jnp.int32)
    slot_peer = jnp.repeat(peers[:, :PAIR_GRP // CAP], CAP, axis=1)
    order_scores = jax.random.randint(key_order, (groups, PAIR_GRP), 0, 1 << 20) * PAIR_GRP + jnp.arange(PAIR_GRP)[None, :]
    order = jnp.argsort(order_scores, axis=1)
    slot_peer = jnp.take_along_axis(slot_peer, order, axis=1)
    right = slot_peer * BLK_GRP + jax.random.randint(key_right, (groups, PAIR_GRP), 0, BLK_GRP)
    left = jnp.arange(groups)[:, None] * BLK_GRP + jax.random.randint(key_left, (groups, PAIR_GRP), 0, BLK_GRP)
    return (left.reshape(-1).astype(jnp.int32), right.reshape(-1).astype(jnp.int32))


def draw_pair_left(key, part):
    return pair_tables(key)[0]


def draw_pair_right(key, part):
    return pair_tables(key)[1]


def set_ends(values, stream_key, least, high):
    index_at = [jax.random.randint(jax.random.fold_in(stream_key, axis), (), 0, length) for axis, length in enumerate(values.shape)]
    longest = values.shape.index(max(values.shape))
    beside = index_at[:longest] + [(index_at[longest] + 1) % values.shape[longest]] + index_at[longest + 1:]
    return values.at[tuple(index_at)].set(least).at[tuple(beside)].set(high)


def block_levels(stream_key, extent, cuts, low, top_value):
    gain = 1.0
    for position, shards_of in cuts:
        draws = jax.random.uniform(jax.random.fold_in(jax.random.fold_in(stream_key, 6), position), (shards_of,), jnp.float32, low / len(cuts), top_value / len(cuts))
        gain = gain * jnp.repeat(jnp.exp(draws), extent[position] // shards_of).reshape((-1,) + (1,) * (len(extent) - 1 - position))
    return gain


def rank_table(number_of, slope):
    loads = [(1 << 20) // math.isqrt(rank ** slope) + 1 for rank in range(1, number_of + 1)]
    deviation = 1 + sum(loads) // (1 << 30)
    return np.cumsum(np.array([max(1, weight // deviation) for weight in loads]))


def ranked_ids(stream_key, shape, count, skew):
    listing = rank_table(count, skew)
    lot = jax.random.randint(jax.random.fold_in(stream_key, 1), shape, 0, int(listing[count - 1]))
    grade = jnp.searchsorted(jnp.asarray(listing, jnp.int32), lot, side="right")
    return jax.random.permutation(jax.random.fold_in(stream_key, 2), count)[grade].astype(jnp.int32)


def normal_values(key, dims, spread, reach, cuts=(), dtype=jnp.bfloat16):
    entries = spread * jax.random.normal(key, dims, jnp.float32)
    if cuts:
        entries = entries * block_levels(key, dims, cuts, -0.22, 0.18)
    return jnp.clip(entries, -reach, reach).astype(dtype)


def setup_inputs(seed: int = 0) -> dict:
    key_list = jax.random.split(jax.random.key(seed), 6)
    embeddings = normal_values(key_list[0], (NBLK, BR, DIM), 1.0, 6.0, ((0, 64), (1, 4)))
    cluster_ids = set_ends(ranked_ids(key_list[1], (NBLK, BR), CLUSTERS, 2), jax.random.fold_in(key_list[1], 3), 0, CLUSTERS - 1).astype(jnp.int32)
    valid = set_ends((jax.random.randint(key_list[2], (NBLK, BR), 0, 8) < 7).astype(jnp.int32), jax.random.fold_in(key_list[2], 1), 0, 1)
    pair_left = draw_pair_left(jax.random.fold_in(key_list[5], 71), 0)
    pair_right = draw_pair_right(jax.random.fold_in(key_list[5], 71), 0)
    return {"embeddings": embeddings, "cluster_ids": cluster_ids, "valid": valid, "pair_left": pair_left, "pair_right": pair_right}


def reference(embeddings, cluster_ids, valid, pair_left, pair_right):
    wide_rows = embeddings.astype(jnp.float32)
    unit = (wide_rows * lax.rsqrt(lax.optimization_barrier(jnp.sum(wide_rows * wide_rows, axis=-1, keepdims=True)) + 1e-06)).astype(jnp.bfloat16)
    labels = jnp.where(valid > 0, cluster_ids, -1).astype(jnp.int32)
    row_ids = jnp.arange(BR)
    batch = math.gcd(PAIRS, 8)
    lefts = pair_left.reshape(-1, batch).astype(jnp.int32)
    rights = pair_right.reshape(-1, batch).astype(jnp.int32)

    def visit(best, picks):
        left_pick, right_pick = picks
        left_rows = unit[left_pick].astype(jnp.float32)
        right_rows = unit[right_pick].astype(jnp.float32)
        scores = jnp.einsum('bid,bjd->bij', left_rows, right_rows, precision=lax.Precision.HIGHEST)
        left_tags = labels[left_pick]
        right_tags = labels[right_pick]
        keep = (left_tags[:, :, None] == right_tags[:, None, :]) & (left_tags[:, :, None] >= 0)
        diagonal = (left_pick == right_pick)[:, None, None] & (row_ids[None, :, None] == row_ids[None, None, :])
        masked = jnp.where(keep & ~diagonal, scores, jnp.float32(-1.0))
        best = best.at[left_pick].max(lax.optimization_barrier(jnp.max(masked, axis=2)))
        best = best.at[right_pick].max(lax.optimization_barrier(jnp.max(masked, axis=1)))
        return (best, None)
    start = jnp.full((NBLK, BR), -1.0, jnp.float32)
    best, _ = lax.scan(visit, start, (lefts, rights))
    return best
```

```python
import jax
import jax.numpy as jnp
from jax import lax
from jax.experimental import pallas as pl
from jax.experimental.pallas import tpu as pltpu
from jax.sharding import Mesh, PartitionSpec as P

epsilon = 1e-06
ROWS = 128
BLOCKS = 4
META = 16
HALF1 = 2 * ROWS + META
HALF2 = 2 * ROWS
FULL = HALF1 + HALF2
SLOTS = 4


def unit_kernel(emb_ref, meta_ref, out_ref):
    for block in range(BLOCKS):
        rows = emb_ref[block].astype(jnp.float32)
        scale = lax.rsqrt(jnp.sum(rows * rows, axis=-1, keepdims=True) + epsilon)
        start = block * ROWS + (META if block >= 2 else 0)
        out_ref[start : start + ROWS, :] = (rows * scale).astype(jnp.bfloat16)
    out_ref[2 * ROWS : HALF1, :] = meta_ref[...]


def choose(index, low, high, act):
    if high - low == 1:
        act(low)
        return
    mid = (low + high) // 2

    @pl.when(index < mid)
    def _():
        choose(index, low, mid, act)

    @pl.when(index >= mid)
    def _():
        choose(index, mid, high, act)


def pair_kernel(left_at, right_at, table, place, left_tags, right_tags, *rest):
    n_refs = 1 + max(max(r for pair in left_at for r, _ in pair), max(r for pair in right_at for r, _ in pair))
    refs = rest[:n_refs]
    left_out, right_out, todo, left_buf, right_buf, sems = rest[n_refs:]
    left_out[...] = jnp.full(left_out.shape, -1.0, jnp.float32)
    right_out[...] = jnp.full(right_out.shape, -1.0, jnp.float32)

    def note(s, n):
        todo[n] = s
        return n + jnp.where(table[s] > 0, 1, 0)

    count = lax.fori_loop(0, 64, note, 0)

    def parse(i):
        s = todo[i]
        code = table[s] - 1
        return s // 4, s % 4, code // 4, code % 4

    def start(i):
        slot = lax.rem(i, SLOTS)
        chunk, dx, a, b = parse(i)

        def fetch_left(k, half):
            ref, base = left_at[k][half]
            row = base + (a - 2 * half) * ROWS
            pltpu.make_async_copy(refs[ref].at[pl.ds(pl.multiple_of(row, 16), ROWS), :], left_buf.at[slot], sems.at[slot, 4]).start()

        def fetch_right(k, half):
            for dy in range(4):
                ref, base = right_at[k * 4 + dy][half]
                row = base + (b - 2 * half) * ROWS
                pltpu.make_async_copy(
                    refs[ref].at[pl.ds(pl.multiple_of(row, 16), ROWS), :],
                    right_buf.at[slot, pl.ds(dy * ROWS, ROWS), :],
                    sems.at[slot, dy],
                ).start()

        choose(chunk * 2 + a // 2, 0, 32, lambda j: fetch_left(j // 2, j % 2))
        choose(dx * 2 + b // 2, 0, 8, lambda j: fetch_right(j // 2, j % 2))

    def finish(i):
        slot = lax.rem(i, SLOTS)
        pltpu.make_async_copy(left_buf.at[slot], left_buf.at[slot], sems.at[slot, 4]).wait()
        for dy in range(4):
            part = right_buf.at[slot, pl.ds(dy * ROWS, ROWS), :]
            pltpu.make_async_copy(part, part, sems.at[slot, dy]).wait()

    for i in range(SLOTS):

        @pl.when(i < count)
        def _(i=i):
            start(jnp.int32(i))

    row_ids = lax.broadcasted_iota(jnp.int32, (ROWS, ROWS), 0)
    col_ids = lax.broadcasted_iota(jnp.int32, (ROWS, ROWS), 1)
    my_z, my_x, my_c, my_y = place[0], place[1], place[2], place[3]

    def step(i, carry):
        slot = lax.rem(i, SLOTS)
        chunk, dx, a, b = parse(i)
        finish(i)
        scores = lax.dot_general(
            left_buf[slot], right_buf[slot], (((1,), (1,)), ((), ())), preferred_element_type=jnp.float32
        )
        tags = jnp.broadcast_to(left_tags[pl.ds(chunk * 4 + a, 1), :], (ROWS, ROWS)).T
        selfish = (chunk == 0) & (dx == 0) & (a == b)
        best = None
        right_x = lax.rem(my_x + dx, 4)
        for dy in range(4):
            keep = tags == right_tags[pl.ds((dx * 4 + dy) * 4 + b, 1), :]
            if dy == 0:
                keep = keep & ((row_ids != col_ids) | jnp.logical_not(selfish))
            masked = jnp.where(keep, scores[:, dy * ROWS : (dy + 1) * ROWS], -1.0)
            best = masked if best is None else jnp.maximum(best, masked)
            row = (right_x * 4 + lax.rem(my_y + dy, 4)) * 4 + b
            right_out[pl.ds(row, 1), :] = jnp.maximum(right_out[pl.ds(row, 1), :], jnp.max(masked, axis=0, keepdims=True))
        left_z = lax.rem(my_z + chunk // 2, 8)
        left_c = lax.rem(my_c + chunk, 2)
        row = (left_z * 2 + left_c) * 4 + a
        left_out[pl.ds(row, 1), :] = jnp.maximum(left_out[pl.ds(row, 1), :], jnp.max(best.T, axis=0, keepdims=True))

        @pl.when(i + SLOTS < count)
        def _():
            start(i + SLOTS)

        return carry

    lax.fori_loop(0, count, step, 0)


def shift(value, axis, by):
    size = lax.axis_size(axis)
    return lax.ppermute(value, axis, [((i + by) % size, i) for i in range(size)])


def local(embeddings, cluster_ids, valid, pair_left, pair_right):
    my_z, my_x, my_c, my_y = (lax.axis_index(name) for name in ("z", "x", "c", "y"))
    labels = jnp.where(valid > 0, cluster_ids, -1).reshape(1, -1)
    meta = jnp.concatenate([labels, (pair_left % BLOCKS)[None], pair_right[None]], axis=1).astype(jnp.bfloat16)
    meta = jnp.pad(meta, ((0, META - 1), (0, 1024 - meta.shape[1])))
    own = pl.pallas_call(unit_kernel, out_shape=jax.ShapeDtypeStruct((FULL, 1024), jnp.bfloat16), name="unit_rows")(embeddings, meta)

    def halves(value):
        return value[:HALF1], value[HALF1:]

    def ring(value, axis):
        up, down = shift(value, axis, 1), shift(value, axis, -1)
        return up, down

    column = {0: halves(own)}
    near = {}
    h_up, h_down = [halves(own)[0], halves(own)[1]], [halves(own)[0], halves(own)[1]]
    for step in (1, 2, 3):
        for h in (0, 1):
            h_up[h], h_down[h] = shift(h_up[h], "z", 1), shift(h_down[h], "z", -1)
        column[step], column[8 - step] = tuple(h_up), tuple(h_down)
    column[4] = (shift(h_up[0], "z", 1), shift(h_down[1], "z", -1))
    left = []
    for dz in range(8):
        mine = column[dz]
        if dz == 0:
            full = shift(own, "c", 1)
            left += [mine, halves(full)]
        else:
            left += [mine, tuple(shift(v, "c", 1) for v in mine)]

    plane = {(0, 0): halves(own)}
    xs = {1: shift(own, "x", 1), 3: shift(own, "x", -1)}
    ys = {1: shift(own, "y", 1), 3: shift(own, "y", -1)}
    for d in (1, 3):
        plane[d, 0], plane[0, d] = halves(xs[d]), halves(ys[d])
    plane[2, 0] = (shift(plane[1, 0][0], "x", 1), shift(plane[3, 0][1], "x", -1))
    plane[0, 2] = (shift(plane[0, 1][0], "y", 1), shift(plane[0, 3][1], "y", -1))
    first, second = {}, {}
    for d in (1, 3):
        for s, by in ((1, 1), (3, -1)):
            first[d, s] = shift(plane[d, 0][0], "y", by)
            second[s, d] = shift(plane[0, d][1], "x", by)
    for s, by in ((1, 1), (3, -1)):
        first[2, s] = shift(plane[2, 0][0], "y", by)
        second[s, 2] = shift(plane[0, 2][1], "x", by)
    first[1, 2], first[3, 2] = shift(first[1, 1], "y", 1), shift(first[3, 3], "y", -1)
    second[2, 1], second[2, 3] = shift(second[1, 1], "x", 1), shift(second[3, 3], "x", -1)
    first[2, 2] = (shift(first[2, 1][:ROWS], "y", 1), shift(first[2, 3][ROWS:], "y", -1))
    first[2, 2] = jnp.concatenate(first[2, 2])
    second[2, 2] = (shift(second[1, 2][:ROWS], "x", 1), shift(second[3, 2][ROWS:], "x", -1))
    second[2, 2] = jnp.concatenate(second[2, 2])
    right = []
    for dx in range(4):
        for dy in range(4):
            if dx and dy:
                right.append((first[dx, dy], second[dx, dy]))
            else:
                right.append(plane[dx, dy])

    left_meta = jnp.stack([h1[2 * ROWS, :].astype(jnp.float32) for h1, _ in left])
    right_meta = jnp.stack([h1[2 * ROWS, :512].astype(jnp.float32) for h1, _ in right])
    left_tags = left_meta[:, :512].reshape(64, ROWS)
    right_tags = right_meta.reshape(64, ROWS)
    right_tags = jnp.where(right_tags < 0, -2.0, right_tags)
    listed = left_meta[:, 512:576].astype(jnp.int32)
    a, b = listed[:, :32], listed[:, 32:]
    group = b // BLOCKS
    mine = (group // 8 == my_z) & (group % 2 == my_c)
    dx = ((group // 2) % 4 - my_x) % 4
    code = jnp.where(mine, 1 + a * BLOCKS + b % BLOCKS, 0)
    table = jnp.max(jnp.where(dx[:, :, None] == jnp.arange(4), code[:, :, None], 0), axis=1).reshape(64)
    place = jnp.stack([my_z, my_x, my_c, my_y]).astype(jnp.int32)

    operands, left_at, right_at = [], [], []
    for source, into in ((left, left_at), (right, right_at)):
        for h1, h2 in source:
            into.append(((len(operands), 0), (len(operands) + 1, 0)))
            operands += [h1, h2]

    def kernel(*refs):
        pair_kernel(left_at, right_at, *refs)

    smem, vmem = pl.BlockSpec(memory_space=pltpu.SMEM), pl.BlockSpec(memory_space=pltpu.VMEM)
    left_best, right_best = pl.pallas_call(
        kernel,
        out_shape=(jax.ShapeDtypeStruct((64, ROWS), jnp.float32),) * 2,
        in_specs=[smem, smem, vmem, vmem] + [pl.BlockSpec(memory_space=pl.ANY)] * len(operands),
        out_specs=(vmem, vmem),
        scratch_shapes=[
            pltpu.SMEM((65,), jnp.int32),
            pltpu.VMEM((SLOTS, ROWS, 1024), jnp.bfloat16),
            pltpu.VMEM((SLOTS, 4 * ROWS, 1024), jnp.bfloat16),
            pltpu.SemaphoreType.DMA((SLOTS, 5)),
        ],
        compiler_params=pltpu.CompilerParams(vmem_limit_bytes=16 * 1024 * 1024),
        name="pair_maxima",
    )(table, place, left_tags, right_tags, *operands)
    from_left = lax.all_to_all(left_best.reshape(16, BLOCKS, ROWS), ("z", "c"), 0, 0, tiled=True)
    from_right = lax.all_to_all(right_best.reshape(16, BLOCKS, ROWS), ("x", "y"), 0, 0, tiled=True)
    return jnp.maximum(jnp.max(from_left, axis=0), jnp.max(from_right, axis=0))


def solution(mesh):
    wide = Mesh(mesh.devices.reshape(8, 4, 2, 4), ("z", "x", "c", "y"))
    dp = ("z", "x", "c")
    placed = (P(dp, "y", None), P(dp, "y"), P(dp, "y"), P(dp), P(dp))
    return jax.shard_map(local, mesh=wide, in_specs=placed, out_specs=P(dp, "y"), check_vma=False)
```

```python
import jax
import jax.numpy as jnp
from jax import lax
from jax.experimental import pallas as pl
from jax.experimental.pallas import tpu as pltpu
from jax.sharding import Mesh, PartitionSpec as P

epsilon = 1e-06
ROWS = 128
BLOCKS = 4
META = 16
HALF1 = 2 * ROWS + META
HALF2 = 2 * ROWS
EARLY = 3 * ROWS + META
SLOTS = 4
DEPTH = 5
VMEM_LIMIT = 12 * 1024 * 1024


def unit_kernel(emb_ref, meta_ref, early_ref, late_ref, first_ref, second_ref):
    for block in range(BLOCKS):
        rows = emb_ref[block].astype(jnp.float32)
        scale = lax.rsqrt(jnp.sum(rows * rows, axis=-1, keepdims=True) + epsilon)
        unit = (rows * scale).astype(jnp.bfloat16)
        low = block * ROWS
        if block < 3:
            at = low + (META if block == 2 else 0)
            early_ref[at : at + ROWS, :] = unit
        else:
            late_ref[...] = unit
        if block < 2:
            first_ref[low : low + ROWS, :] = unit
        else:
            second_ref[low - 2 * ROWS : low - ROWS, :] = unit
    early_ref[2 * ROWS : HALF1, :] = meta_ref[...]
    first_ref[2 * ROWS : HALF1, :] = meta_ref[...]


def choose(index, low, high, act):
    if high - low == 1:
        act(low)
        return
    mid = (low + high) // 2

    @pl.when(index < mid)
    def _():
        choose(index, low, mid, act)

    @pl.when(index >= mid)
    def _():
        choose(index, mid, high, act)


def pair_kernel(low, high, right_at, table, place, left_tags, right_tags, *rest):
    left_ref, refs = rest[0], rest[1:-8]
    left_in, right_in, left_out, right_out, todo, left_buf, right_buf, sems = rest[-8:]
    left_out[...] = left_in[...]
    right_out[...] = right_in[...]
    per_chunk = left_ref.shape[0] // 16

    def note(s, n):
        todo[n] = s
        code = table[s]
        return n + jnp.where((code > low * 4) & (code <= high * 4), 1, 0)

    count = lax.fori_loop(0, 64, note, 0)

    def parse(i):
        s = todo[i]
        code = table[s] - 1
        return s // 4, s % 4, code // 4, code % 4

    def start(i):
        slot = lax.rem(i, SLOTS)
        chunk, dx, a, b = parse(i)
        row = chunk * per_chunk + (a - low) * ROWS
        if low == 0:
            row = row + jnp.where(a >= 2, META, 0)
        pltpu.make_async_copy(left_ref.at[pl.ds(pl.multiple_of(row, 16), ROWS), :], left_buf.at[slot], sems.at[slot, 4]).start()

        def fetch_right(leaf):
            for dy in range(4):
                ref, base = right_at[leaf // 4 * 4 + dy][leaf % 4]
                pltpu.make_async_copy(
                    refs[ref].at[pl.ds(base, ROWS), :], right_buf.at[slot, pl.ds(dy * ROWS, ROWS), :], sems.at[slot, dy]
                ).start()

        choose(dx * 4 + b, 0, 16, fetch_right)

    def finish(i):
        slot = lax.rem(i, SLOTS)
        pltpu.make_async_copy(left_buf.at[slot], left_buf.at[slot], sems.at[slot, 4]).wait()
        for dy in range(4):
            part = right_buf.at[slot, pl.ds(dy * ROWS, ROWS), :]
            pltpu.make_async_copy(part, part, sems.at[slot, dy]).wait()

    for i in range(SLOTS):

        @pl.when(i < count)
        def _(i=i):
            start(jnp.int32(i))

    row_ids = lax.broadcasted_iota(jnp.int32, (ROWS, ROWS), 0)
    col_ids = lax.broadcasted_iota(jnp.int32, (ROWS, ROWS), 1)
    my_z, my_x, my_c, my_y = place[0], place[1], place[2], place[3]

    def step(i, carry):
        slot = lax.rem(i, SLOTS)
        chunk, dx, a, b = parse(i)
        finish(i)
        scores = lax.dot_general(
            left_buf[slot], right_buf[slot], (((1,), (1,)), ((), ())), preferred_element_type=jnp.float32
        )
        tags = jnp.broadcast_to(left_tags[pl.ds(chunk * 4 + a, 1), :], (ROWS, ROWS)).T
        selfish = (chunk == my_z * 2 + my_c) & (dx == 0) & (a == b)
        best = None
        right_x = lax.rem(my_x + dx, 4)
        for dy in range(4):
            keep = tags == right_tags[pl.ds((dx * 4 + dy) * 4 + b, 1), :]
            if dy == 0:
                keep = keep & ((row_ids != col_ids) | jnp.logical_not(selfish))
            masked = jnp.where(keep, scores[:, dy * ROWS : (dy + 1) * ROWS], -1.0)
            best = masked if best is None else jnp.maximum(best, masked)
            row = (right_x * 4 + lax.rem(my_y + dy, 4)) * 4 + b
            right_out[pl.ds(row, 1), :] = jnp.maximum(right_out[pl.ds(row, 1), :], jnp.max(masked, axis=0, keepdims=True))
        row = chunk * 4 + a
        left_out[pl.ds(row, 1), :] = jnp.maximum(left_out[pl.ds(row, 1), :], jnp.max(best.T, axis=0, keepdims=True))

        @pl.when(i + SLOTS < count)
        def _():
            start(i + SLOTS)

        return carry

    lax.fori_loop(0, count, step, 0)


class Carrier:
    def __init__(self):
        self.sent = []

    def __call__(self, value, axis, by):
        if len(self.sent) >= DEPTH:
            k = len(self.sent) - DEPTH
            value, self.sent[k][0] = lax.optimization_barrier((value, self.sent[k][0]))
        size = lax.axis_size(axis)
        cell = [lax.ppermute(value, axis, [((i + by) % size, i) for i in range(size)])]
        self.sent.append(cell)
        return cell


def gather_plane(h1, h2):
    send = Carrier()
    xp, xm, yp, ym = [], [], [], []
    order = ((xp, "x", 1), (xm, "x", -1), (yp, "y", 1), (ym, "y", -1))

    def send_all(values):
        for (into, axis, by), value in zip(order, values):
            into.append(send(value[0], axis, by))

    own1, own2 = [h1], [h2]
    send_all((own1, own2, own1, own2))
    send_all((own2, own1, own2, own1))
    x1, x3 = (xp[0], xp[1]), (xm[1], xm[0])
    y1, y3 = (yp[0], yp[1]), (ym[1], ym[0])
    send_all((x1[0], x3[1], y1[0], y3[1]))
    x2, y2 = (xp[2], xm[2]), (yp[2], ym[2])
    send_all((y1[1], y1[1], x1[0], x1[0]))
    send_all((y3[1], y3[1], x3[0], x3[0]))
    send_all((y2[1], y2[1], x2[0], x2[0]))
    send_all((xp[3], xm[4], yp[3], ym[4]))
    low, high = [xp[5][0][:ROWS]], [xm[5][0][ROWS:]]
    low_y, high_y = [yp[5][0][:ROWS]], [ym[5][0][ROWS:]]
    send_all((low, high, low_y, high_y))
    second = {(1, 1): xp[3], (3, 1): xm[3], (1, 3): xp[4], (3, 3): xm[4], (1, 2): xp[5], (3, 2): xm[5], (2, 1): xp[6], (2, 3): xm[6]}
    first = {(1, 1): yp[3], (1, 3): ym[3], (3, 1): yp[4], (3, 3): ym[4], (2, 1): yp[5], (2, 3): ym[5], (1, 2): yp[6], (3, 2): ym[6]}
    whole = {(0, 0): (own1, own2), (1, 0): x1, (3, 0): x3, (2, 0): x2, (0, 1): y1, (0, 3): y3, (0, 2): y2}
    for key in first:
        whole[key] = (first[key], second[key])
    parts = {}
    for key, (a, b) in whole.items():
        parts[key] = ((a[0], 0), (a[0], ROWS), (b[0], 0), (b[0], ROWS))
    parts[2, 2] = ((yp[7][0], 0), (ym[7][0], 0), (xp[7][0], 0), (xm[7][0], 0))
    metas = {key: (a[0], 2 * ROWS) for key, (a, _) in whole.items()}
    metas[2, 2] = (ym[7][0], ROWS)
    return parts, metas


def local(embeddings, cluster_ids, valid, pair_left, pair_right):
    my_z, my_x, my_c, my_y = (lax.axis_index(name) for name in ("z", "x", "c", "y"))
    labels = jnp.where(valid > 0, cluster_ids, -1).reshape(1, -1)
    meta = jnp.concatenate([labels, (pair_left % BLOCKS)[None], pair_right[None]], axis=1).astype(jnp.bfloat16)
    meta = jnp.pad(meta, ((0, META - 1), (0, 1024 - meta.shape[1])))
    shapes = [jax.ShapeDtypeStruct((n, 1024), jnp.bfloat16) for n in (EARLY, ROWS, HALF1, HALF2)]
    early, late, h1, h2 = pl.pallas_call(unit_kernel, out_shape=shapes, name="unit_rows")(embeddings, meta)
    left_early = lax.all_gather(early, ("z", "c"), axis=0, tiled=True)
    left_late = lax.all_gather(late, ("z", "c"), axis=0, tiled=True)
    parts, metas = gather_plane(h1, h2)

    left_meta = left_early.reshape(16, EARLY, 1024)[:, 2 * ROWS, :576].astype(jnp.float32)
    keys = [(dx, dy) for dx in range(4) for dy in range(4)]
    right_meta = jnp.stack([metas[k][0][metas[k][1], :512] for k in keys]).astype(jnp.float32)
    left_tags = left_meta[:, :512].reshape(64, ROWS)
    right_tags = right_meta.reshape(64, ROWS)
    right_tags = jnp.where(right_tags < 0, -2.0, right_tags)
    listed = left_meta[:, 512:576].astype(jnp.int32)
    a, b = listed[:, :32], listed[:, 32:]
    group = b // BLOCKS
    mine = (group // 8 == my_z) & (group % 2 == my_c)
    dx = ((group // 2) % 4 - my_x) % 4
    code = jnp.where(mine, 1 + a * BLOCKS + b % BLOCKS, 0)
    table = jnp.max(jnp.where(dx[:, :, None] == jnp.arange(4), code[:, :, None], 0), axis=1).reshape(64)
    place = jnp.stack([my_z, my_x, my_c, my_y]).astype(jnp.int32)

    operands, known, right_at = [], {}, []
    for k in keys:
        row = []
        for value, base in parts[k]:
            if id(value) not in known:
                known[id(value)] = len(operands)
                operands.append(value)
            row.append((known[id(value)], base))
        right_at.append(row)

    smem, vmem = pl.BlockSpec(memory_space=pltpu.SMEM), pl.BlockSpec(memory_space=pltpu.VMEM)

    def maxima(low, high, left_rows, before):
        def kernel(*refs):
            pair_kernel(low, high, right_at, *refs)

        return pl.pallas_call(
            kernel,
            out_shape=(jax.ShapeDtypeStruct((64, ROWS), jnp.float32),) * 2,
            in_specs=[smem, smem, vmem, vmem, pl.BlockSpec(memory_space=pltpu.HBM)] + [vmem] * (len(operands) + 2),
            out_specs=(vmem, vmem),
            scratch_shapes=[
                pltpu.SMEM((65,), jnp.int32),
                pltpu.VMEM((SLOTS, ROWS, 1024), jnp.bfloat16),
                pltpu.VMEM((SLOTS, 4 * ROWS, 1024), jnp.bfloat16),
                pltpu.SemaphoreType.DMA((SLOTS, 5)),
            ],
            compiler_params=pltpu.CompilerParams(vmem_limit_bytes=VMEM_LIMIT),
            name="pair_maxima",
        )(table, place, left_tags, right_tags, left_rows, *operands, *before)

    none = jnp.full((64, ROWS), -1.0, jnp.float32)
    before = maxima(0, 3, left_early, (none, none))
    left_best, right_best = maxima(3, 4, left_late, before)
    from_left = lax.all_to_all(left_best.reshape(16, BLOCKS, ROWS), ("z", "c"), 0, 0, tiled=True)
    from_right = lax.all_to_all(right_best.reshape(16, BLOCKS, ROWS), ("x", "y"), 0, 0, tiled=True)
    return jnp.maximum(jnp.max(from_left, axis=0), jnp.max(from_right, axis=0))


def solution(mesh):
    wide = Mesh(mesh.devices.reshape(8, 4, 2, 4), ("z", "x", "c", "y"))
    dp = ("z", "x", "c")
    placed = (P(dp, "y", None), P(dp, "y"), P(dp, "y"), P(dp), P(dp))
    return jax.shard_map(local, mesh=wide, in_specs=placed, out_specs=P(dp, "y"), check_vma=False)
```

```python
import jax
import jax.numpy as jnp
from jax import lax
from jax.experimental import pallas as pl
from jax.experimental.pallas import tpu as pltpu
from jax.sharding import Mesh, PartitionSpec as P

epsilon = 1e-06
ROWS = 128
BLOCKS = 4
META = 16
HALF1 = 2 * ROWS + META
HALF2 = 2 * ROWS
FULL = HALF1 + HALF2
SLOTS = 4
DEPTH = 5
VMEM_LIMIT = 12 * 1024 * 1024


def unit_kernel(emb_ref, meta_ref, full_ref, first_ref, second_ref):
    for block in range(BLOCKS):
        rows = emb_ref[block].astype(jnp.float32)
        scale = lax.rsqrt(jnp.sum(rows * rows, axis=-1, keepdims=True) + epsilon)
        unit = (rows * scale).astype(jnp.bfloat16)
        low = block * ROWS
        at = low + (META if block >= 2 else 0)
        full_ref[at : at + ROWS, :] = unit
        if block < 2:
            first_ref[low : low + ROWS, :] = unit
        else:
            second_ref[low - 2 * ROWS : low - ROWS, :] = unit
    full_ref[2 * ROWS : HALF1, :] = meta_ref[...]
    first_ref[2 * ROWS : HALF1, :] = meta_ref[...]


def choose(index, low, high, act):
    if high - low == 1:
        act(low)
        return
    mid = (low + high) // 2

    @pl.when(index < mid)
    def _():
        choose(index, low, mid, act)

    @pl.when(index >= mid)
    def _():
        choose(index, mid, high, act)


def pair_kernel(right_at, meta_at, table, place, left_ref, *rest):
    refs = rest[:-11]
    left_out, right_out, todo, left_buf, right_buf, left_meta, right_meta, left_tags, right_tags, sems, meta_sems = rest[-11:]
    for k in range(16):
        pltpu.make_async_copy(left_ref.at[pl.ds(k * FULL + 2 * ROWS, META), :], left_meta.at[k], meta_sems.at[0]).start()
        ref, row = meta_at[k]
        pltpu.make_async_copy(refs[ref].at[pl.ds(row, META), :], right_meta.at[k], meta_sems.at[1]).start()

    def note(s, n):
        todo[n] = s
        return n + jnp.where(table[s] > 0, 1, 0)

    count = lax.fori_loop(0, 64, note, 0)

    def parse(i):
        s = todo[i]
        code = table[s] - 1
        return s // 4, s % 4, code // 4, code % 4

    def start(i):
        slot = lax.rem(i, SLOTS)
        chunk, dx, a, b = parse(i)
        row = chunk * FULL + a * ROWS + jnp.where(a >= 2, META, 0)
        pltpu.make_async_copy(left_ref.at[pl.ds(pl.multiple_of(row, 16), ROWS), :], left_buf.at[slot], sems.at[slot, 4]).start()

        def fetch_right(leaf):
            for dy in range(4):
                ref, base = right_at[leaf // 4 * 4 + dy][leaf % 4]
                pltpu.make_async_copy(
                    refs[ref].at[pl.ds(base, ROWS), :], right_buf.at[slot, pl.ds(dy * ROWS, ROWS), :], sems.at[slot, dy]
                ).start()

        choose(dx * 4 + b, 0, 16, fetch_right)

    def finish(i):
        slot = lax.rem(i, SLOTS)
        pltpu.make_async_copy(left_buf.at[slot], left_buf.at[slot], sems.at[slot, 4]).wait()
        for dy in range(4):
            part = right_buf.at[slot, pl.ds(dy * ROWS, ROWS), :]
            pltpu.make_async_copy(part, part, sems.at[slot, dy]).wait()

    for i in range(SLOTS):

        @pl.when(i < count)
        def _(i=i):
            start(jnp.int32(i))

    left_out[...] = jnp.full(left_out.shape, -1.0, jnp.float32)
    right_out[...] = jnp.full(right_out.shape, -1.0, jnp.float32)
    pltpu.make_async_copy(left_meta, left_meta, meta_sems.at[0]).wait()
    pltpu.make_async_copy(right_meta, right_meta, meta_sems.at[1]).wait()
    for k in range(16):
        left_row = left_meta[k, 0:1, : 4 * ROWS].astype(jnp.float32)
        right_row = right_meta[k, 0:1, : 4 * ROWS].astype(jnp.float32)
        right_row = jnp.where(right_row < 0.0, -2.0, right_row)
        for block in range(4):
            left_tags[k * 4 + block : k * 4 + block + 1, :] = left_row[:, block * ROWS : (block + 1) * ROWS]
            right_tags[k * 4 + block : k * 4 + block + 1, :] = right_row[:, block * ROWS : (block + 1) * ROWS]

    row_ids = lax.broadcasted_iota(jnp.int32, (ROWS, ROWS), 0)
    col_ids = lax.broadcasted_iota(jnp.int32, (ROWS, ROWS), 1)
    my_z, my_x, my_c, my_y = place[0], place[1], place[2], place[3]

    def step(i, carry):
        slot = lax.rem(i, SLOTS)
        chunk, dx, a, b = parse(i)
        finish(i)
        scores = lax.dot_general(
            left_buf[slot], right_buf[slot], (((1,), (1,)), ((), ())), preferred_element_type=jnp.float32
        )
        tags = jnp.broadcast_to(left_tags[pl.ds(chunk * 4 + a, 1), :], (ROWS, ROWS)).T
        selfish = (chunk == my_z * 2 + my_c) & (dx == 0) & (a == b)
        best = None
        right_x = lax.rem(my_x + dx, 4)
        for dy in range(4):
            keep = tags == right_tags[pl.ds((dx * 4 + dy) * 4 + b, 1), :]
            if dy == 0:
                keep = keep & ((row_ids != col_ids) | jnp.logical_not(selfish))
            masked = jnp.where(keep, scores[:, dy * ROWS : (dy + 1) * ROWS], -1.0)
            best = masked if best is None else jnp.maximum(best, masked)
            row = (right_x * 4 + lax.rem(my_y + dy, 4)) * 4 + b
            right_out[pl.ds(row, 1), :] = jnp.maximum(right_out[pl.ds(row, 1), :], jnp.max(masked, axis=0, keepdims=True))
        row = chunk * 4 + a
        left_out[pl.ds(row, 1), :] = jnp.maximum(left_out[pl.ds(row, 1), :], jnp.max(best.T, axis=0, keepdims=True))

        @pl.when(i + SLOTS < count)
        def _():
            start(i + SLOTS)

        return carry

    lax.fori_loop(0, count, step, 0)


def pair_maxima(table, place, left_rows, operands, right_at, meta_at):
    def kernel(*refs):
        pair_kernel(right_at, meta_at, *refs)

    smem, vmem, hbm = (pl.BlockSpec(memory_space=s) for s in (pltpu.SMEM, pltpu.VMEM, pltpu.HBM))
    return pl.pallas_call(
        kernel,
        out_shape=(jax.ShapeDtypeStruct((64, ROWS), jnp.float32),) * 2,
        in_specs=[smem, smem] + [hbm] * (len(operands) + 1),
        out_specs=(vmem, vmem),
        scratch_shapes=[
            pltpu.SMEM((65,), jnp.int32),
            pltpu.VMEM((SLOTS, ROWS, 1024), jnp.bfloat16),
            pltpu.VMEM((SLOTS, 4 * ROWS, 1024), jnp.bfloat16),
            pltpu.VMEM((16, META, 1024), jnp.bfloat16),
            pltpu.VMEM((16, META, 1024), jnp.bfloat16),
            pltpu.VMEM((64, ROWS), jnp.float32),
            pltpu.VMEM((64, ROWS), jnp.float32),
            pltpu.SemaphoreType.DMA((SLOTS, 5)),
            pltpu.SemaphoreType.DMA((2,)),
        ],
        compiler_params=pltpu.CompilerParams(vmem_limit_bytes=VMEM_LIMIT),
        name="pair_maxima",
    )(table, place, *(pltpu.with_memory_space_constraint(v, pltpu.HBM) for v in (left_rows, *operands)))


class Carrier:
    def __init__(self):
        self.sent = []

    def __call__(self, value, axis, by):
        if len(self.sent) >= DEPTH:
            k = len(self.sent) - DEPTH
            value, self.sent[k][0] = lax.optimization_barrier((value, self.sent[k][0]))
        size = lax.axis_size(axis)
        cell = [lax.ppermute(value, axis, [((i + by) % size, i) for i in range(size)])]
        self.sent.append(cell)
        return cell


def gather_plane(h1, h2):
    send = Carrier()
    xp, xm, yp, ym = [], [], [], []
    order = ((xp, "x", 1), (xm, "x", -1), (yp, "y", 1), (ym, "y", -1))

    def send_all(values):
        for (into, axis, by), value in zip(order, values):
            into.append(send(value[0], axis, by))

    own1, own2 = [h1], [h2]
    send_all((own1, own2, own1, own2))
    send_all((own2, own1, own2, own1))
    x1, x3 = (xp[0], xp[1]), (xm[1], xm[0])
    y1, y3 = (yp[0], yp[1]), (ym[1], ym[0])
    send_all((x1[0], x3[1], y1[0], y3[1]))
    x2, y2 = (xp[2], xm[2]), (yp[2], ym[2])
    send_all((y1[1], y1[1], x1[0], x1[0]))
    send_all((y3[1], y3[1], x3[0], x3[0]))
    send_all((y2[1], y2[1], x2[0], x2[0]))
    send_all((xp[3], xm[4], yp[3], ym[4]))
    low, high = [xp[5][0][:ROWS]], [xm[5][0][ROWS:]]
    low_y, high_y = [yp[5][0][:ROWS]], [ym[5][0][ROWS:]]
    send_all((low, high, low_y, high_y))
    second = {(1, 1): xp[3], (3, 1): xm[3], (1, 3): xp[4], (3, 3): xm[4], (1, 2): xp[5], (3, 2): xm[5], (2, 1): xp[6], (2, 3): xm[6]}
    first = {(1, 1): yp[3], (1, 3): ym[3], (3, 1): yp[4], (3, 3): ym[4], (2, 1): yp[5], (2, 3): ym[5], (1, 2): yp[6], (3, 2): ym[6]}
    whole = {(0, 0): (own1, own2), (1, 0): x1, (3, 0): x3, (2, 0): x2, (0, 1): y1, (0, 3): y3, (0, 2): y2}
    for key in first:
        whole[key] = (first[key], second[key])
    parts = {}
    for key, (a, b) in whole.items():
        parts[key] = ((a[0], 0), (a[0], ROWS), (b[0], 0), (b[0], ROWS))
    parts[2, 2] = ((yp[7][0], 0), (ym[7][0], 0), (xp[7][0], 0), (xm[7][0], 0))
    metas = {key: (a[0], 2 * ROWS) for key, (a, _) in whole.items()}
    metas[2, 2] = (ym[7][0], ROWS)
    return parts, metas


def local(embeddings, cluster_ids, valid, pair_left, pair_right):
    my_z, my_x, my_c, my_y = (lax.axis_index(name) for name in ("z", "x", "c", "y"))
    labels = jnp.where(valid > 0, cluster_ids, -1).reshape(1, -1)
    meta = jnp.concatenate([labels, (pair_left % BLOCKS)[None], pair_right[None]], axis=1).astype(jnp.bfloat16)
    meta = jnp.pad(meta, ((0, META - 1), (0, 1024 - meta.shape[1])))
    full, h1, h2 = pl.pallas_call(
        unit_kernel,
        out_shape=[jax.ShapeDtypeStruct((n, 1024), jnp.bfloat16) for n in (FULL, HALF1, HALF2)],
        compiler_params=pltpu.CompilerParams(vmem_limit_bytes=VMEM_LIMIT),
        name="unit_rows",
    )(embeddings, meta)
    left_rows = lax.all_gather(full, ("z", "c"), axis=0, tiled=True)
    parts, metas = gather_plane(h1, h2)

    listed = left_rows.reshape(16, FULL, 1024)[:, 2 * ROWS, 512:576].astype(jnp.int32)
    a, b = listed[:, :32], listed[:, 32:]
    group = b // BLOCKS
    mine = (group // 8 == my_z) & (group % 2 == my_c)
    dx = ((group // 2) % 4 - my_x) % 4
    code = jnp.where(mine, 1 + a * BLOCKS + b % BLOCKS, 0)
    table = jnp.max(jnp.where(dx[:, :, None] == jnp.arange(4), code[:, :, None], 0), axis=1).reshape(64)
    place = jnp.stack([my_z, my_x, my_c, my_y]).astype(jnp.int32)

    operands, known, right_at, meta_at = [], {}, [], []

    def place_of(value):
        if id(value) not in known:
            known[id(value)] = len(operands)
            operands.append(value)
        return known[id(value)]

    for k in [(dx, dy) for dx in range(4) for dy in range(4)]:
        right_at.append([(place_of(value), base) for value, base in parts[k]])
        meta_at.append((place_of(metas[k][0]), metas[k][1]))
    left_best, right_best = pair_maxima(table, place, left_rows, operands, right_at, meta_at)
    from_left = lax.all_to_all(left_best.reshape(16, BLOCKS, ROWS), ("z", "c"), 0, 0, tiled=True)
    from_right = lax.all_to_all(right_best.reshape(16, BLOCKS, ROWS), ("x", "y"), 0, 0, tiled=True)
    return jnp.maximum(jnp.max(from_left, axis=0), jnp.max(from_right, axis=0))


def solution(mesh):
    wide = Mesh(mesh.devices.reshape(8, 4, 2, 4), ("z", "x", "c", "y"))
    dp = ("z", "x", "c")
    placed = (P(dp, "y", None), P(dp, "y"), P(dp, "y"), P(dp), P(dp))
    return jax.shard_map(local, mesh=wide, in_specs=placed, out_specs=P(dp, "y"), check_vma=False)
```

```python
import jax
import jax.numpy as jnp
from jax import lax
from jax.experimental import pallas as pl
from jax.experimental.pallas import tpu as pltpu
from jax.sharding import Mesh, PartitionSpec as P

epsilon = 1e-06
ROWS = 128
BLOCKS = 4
META = 16
HALF1 = 2 * ROWS + META
HALF2 = 2 * ROWS
FULL = HALF1 + HALF2
SLOTS = 8
DEPTH = 5
VMEM_LIMIT = 32 * 1024 * 1024


def unit_kernel(emb_ref, meta_ref, unit_ref, full_ref):
    for block in range(BLOCKS):
        rows = emb_ref[block].astype(jnp.float32)
        scale = lax.rsqrt(jnp.sum(rows * rows, axis=-1, keepdims=True) + epsilon)
        unit = (rows * scale).astype(jnp.bfloat16)
        unit_ref[block * ROWS : (block + 1) * ROWS, :] = unit
        at = block * ROWS + (META if block >= 2 else 0)
        full_ref[at : at + ROWS, :] = unit
    full_ref[2 * ROWS : HALF1, :] = meta_ref[...]


def pair_kernel(right_at, meta_at, todo, first, place, left_tags, left_ref, *rest):
    refs = rest[:-10]
    left_out, right_out, left_buf, right_buf, right_meta, tags_buf, best_buf, left_best, left_sems, right_sems = rest[-10:]

    def fetch_right(j):
        for dy in range(4):
            ref, base = right_at[j // 4 * 4 + dy][j % 4]
            pltpu.make_async_copy(
                refs[ref].at[pl.ds(base, ROWS), :], right_buf.at[j, pl.ds(dy * ROWS, ROWS), :], right_sems.at[j]
            ).start()

    for k in range(16):
        ref, row = meta_at[k]
        pltpu.make_async_copy(refs[ref].at[pl.ds(row, META), :], right_meta.at[k], right_sems.at[16]).start()
    for j in range(4):
        fetch_right(j)

    count = first[16]

    def each_left(i, act):
        slot = lax.rem(i, SLOTS)
        for h in range(2):
            unit = todo[2 * i + h]
            into = left_buf.at[slot, pl.ds(h * ROWS, ROWS), :]

            @pl.when(unit < 64)
            def _():
                row = pl.multiple_of(unit * ROWS, ROWS)
                act(pltpu.make_async_copy(left_ref.at[pl.ds(row, ROWS), :], into, left_sems.at[slot, h]))

    def fetch_left(i):
        each_left(i, lambda copy: copy.start())

    def early(i, carry):
        fetch_left(i)
        return carry

    lax.fori_loop(0, jnp.minimum(count, SLOTS), early, 0)
    for j in range(4, 16):
        fetch_right(j)
    left_best[...] = jnp.full(left_best.shape, -1.0, jnp.float32)
    pltpu.make_async_copy(right_meta, right_meta, right_sems.at[16]).wait()

    row_ids = lax.broadcasted_iota(jnp.int32, (ROWS, ROWS), 0)
    col_ids = lax.broadcasted_iota(jnp.int32, (ROWS, ROWS), 1)
    my_z, my_x, my_c, my_y = place[0], place[1], place[2], place[3]
    me = my_z * 2 + my_c

    for j in range(16):
        dx, b = j // 4, j % 4
        for dy in range(4):
            row = right_meta[dx * 4 + dy, 0:1, b * ROWS : (b + 1) * ROWS].astype(jnp.float32)
            row = jnp.where(row < 0.0, -2.0, row)
            tags_buf[dy * ROWS : (dy + 1) * ROWS, :] = jnp.broadcast_to(row, (ROWS, ROWS)).T
        best_buf[...] = jnp.full(best_buf.shape, -1.0, jnp.float32)
        pltpu.make_async_copy(right_buf.at[j], right_buf.at[j], right_sems.at[j]).wait()

        def step(i, carry):
            each_left(i, lambda copy: copy.wait())
            scores = lax.dot_general(
                right_buf[j], left_buf[lax.rem(i, SLOTS)], (((1,), (1,)), ((), ())), preferred_element_type=jnp.float32
            )
            for h in range(2):
                unit = todo[2 * i + h]
                tags = left_tags[pl.ds(unit, 1), :]
                top = None
                for dy in range(4):
                    part = slice(dy * ROWS, (dy + 1) * ROWS)
                    keep = tags_buf[part, :] == tags
                    if dx == 0 and dy == 0:
                        keep = keep & ((row_ids != col_ids) | (unit != me * 4 + b))
                    masked = jnp.where(keep, scores[part, h * ROWS : (h + 1) * ROWS], -1.0)
                    best_buf[part, :] = jnp.maximum(best_buf[part, :], masked)
                    top = masked if top is None else jnp.maximum(top, masked)
                top = jnp.max(top, axis=0, keepdims=True)
                left_best[pl.ds(unit, 1), :] = jnp.maximum(left_best[pl.ds(unit, 1), :], top)

            @pl.when(i + SLOTS < count)
            def _():
                fetch_left(i + SLOTS)

            return carry

        lax.fori_loop(first[j], first[j + 1], step, 0)
        right_x = lax.rem(my_x + dx, 4)
        for dy in range(4):
            row = (right_x * 4 + lax.rem(my_y + dy, 4)) * 4 + b
            right_out[pl.ds(row, 1), :] = jnp.max(best_buf[dy * ROWS : (dy + 1) * ROWS, :].T, axis=0, keepdims=True)
    left_out[...] = left_best[0:64, :]


def pair_maxima(todo, first, place, left_tags, left_rows, operands, right_at, meta_at):
    def kernel(*refs):
        pair_kernel(right_at, meta_at, *refs)

    smem, vmem, hbm = (pl.BlockSpec(memory_space=s) for s in (pltpu.SMEM, pltpu.VMEM, pltpu.HBM))
    return pl.pallas_call(
        kernel,
        out_shape=(jax.ShapeDtypeStruct((64, ROWS), jnp.float32),) * 2,
        in_specs=[smem, smem, smem, vmem] + [hbm] * (len(operands) + 1),
        out_specs=(vmem, vmem),
        scratch_shapes=[
            pltpu.VMEM((SLOTS, 2 * ROWS, 1024), jnp.bfloat16),
            pltpu.VMEM((16, 4 * ROWS, 1024), jnp.bfloat16),
            pltpu.VMEM((16, META, 1024), jnp.bfloat16),
            pltpu.VMEM((4 * ROWS, ROWS), jnp.float32),
            pltpu.VMEM((4 * ROWS, ROWS), jnp.float32),
            pltpu.VMEM((72, ROWS), jnp.float32),
            pltpu.SemaphoreType.DMA((SLOTS, 2)),
            pltpu.SemaphoreType.DMA((17,)),
        ],
        compiler_params=pltpu.CompilerParams(vmem_limit_bytes=VMEM_LIMIT),
        name="pair_maxima",
    )(todo, first, place, left_tags, *(pltpu.with_memory_space_constraint(v, pltpu.HBM) for v in (left_rows, *operands)))


class Carrier:
    def __init__(self):
        self.sent = []

    def __call__(self, value, axis, by):
        if len(self.sent) >= DEPTH:
            k = len(self.sent) - DEPTH
            value, self.sent[k][0] = lax.optimization_barrier((value, self.sent[k][0]))
        size = lax.axis_size(axis)
        cell = [lax.ppermute(value, axis, [((i + by) % size, i) for i in range(size)])]
        self.sent.append(cell)
        return cell


def gather_plane(own, extra):
    send = Carrier()
    xp, xm, yp, ym = ("x", 1), ("x", -1), ("y", 1), ("y", -1)
    whole = {(0, 0): [own]}
    whole[0, 1], whole[0, 3] = send(own, *yp), send(own, *ym)
    whole[1, 0], whole[3, 0] = send(own, *xp), send(own, *xm)
    whole[0, 1][0], extra = lax.optimization_barrier((whole[0, 1][0], extra))
    whole[1, 1] = send(whole[0, 1][0], *xp)
    whole[3, 3] = send(whole[0, 3][0], *xm)
    whole[3, 1] = send(whole[3, 0][0], *yp)
    whole[1, 3] = send(whole[1, 0][0], *ym)
    half = {}
    half["y", 0] = send(whole[0, 1][0][:HALF1], *yp)
    half["y", 1] = send(whole[0, 3][0][HALF1:], *ym)
    half["x", 0] = send(whole[1, 0][0][:HALF1], *xp)
    half["x", 1] = send(whole[3, 0][0][HALF1:], *xm)
    whole[1, 2] = send(whole[1, 1][0], *yp)
    whole[3, 2] = send(whole[3, 3][0], *ym)
    whole[2, 3] = send(whole[1, 3][0], *xp)
    whole[2, 1] = send(whole[3, 1][0], *xm)
    last = [
        send(whole[1, 2][0][:ROWS], *xp),
        send(whole[3, 2][0][ROWS:HALF1], *xm),
        send(whole[2, 3][0][HALF1 : HALF1 + ROWS], *ym),
        send(whole[2, 1][0][HALF1 + ROWS :], *yp),
    ]
    starts = (0, ROWS, HALF1, HALF1 + ROWS)
    parts = {key: [(v[0], at) for at in starts] for key, v in whole.items()}
    metas = {key: (v[0], 2 * ROWS) for key, v in whole.items()}
    for key, axis in (((2, 0), "x"), ((0, 2), "y")):
        h1, h2 = half[axis, 0][0], half[axis, 1][0]
        parts[key] = [(h1, 0), (h1, ROWS), (h2, 0), (h2, ROWS)]
        metas[key] = (h1, 2 * ROWS)
    parts[2, 2] = [(v[0], 0) for v in last]
    metas[2, 2] = (last[1][0], ROWS)
    return parts, metas, extra


def local(embeddings, cluster_ids, valid, pair_left, pair_right):
    my_z, my_x, my_c, my_y = (lax.axis_index(name) for name in ("z", "x", "c", "y"))
    place = jnp.stack([my_z, my_x, my_c, my_y]).astype(jnp.int32)
    labels = jnp.where(valid > 0, cluster_ids, -1).reshape(1, -1)
    lists = jnp.concatenate([labels, (pair_left % BLOCKS)[None], pair_right[None]], axis=1)
    meta = jnp.pad(lists.astype(jnp.bfloat16), ((0, META - 1), (0, 1024 - lists.shape[1])))
    unit, full = pl.pallas_call(
        unit_kernel,
        out_shape=[jax.ShapeDtypeStruct((n, 1024), jnp.bfloat16) for n in (4 * ROWS, FULL)],
        compiler_params=pltpu.CompilerParams(vmem_limit_bytes=VMEM_LIMIT),
        name="unit_rows",
    )(embeddings, meta)
    unit, lists = lax.optimization_barrier((unit, lists))
    left_rows = lax.all_gather(unit, ("z", "c"), axis=0, tiled=True)
    left_lists = lax.all_to_all(jnp.broadcast_to(lists, (16, lists.shape[1])), ("z", "c"), 0, 0, tiled=True)
    parts, metas, left_lists = gather_plane(full, left_lists)

    left_tags = left_lists[:, :512].astype(jnp.float32).reshape(64, ROWS)
    a, b = left_lists[:, 512:544], left_lists[:, 544:]
    group = b // BLOCKS
    mine = (group // 8 == my_z) & (group % 2 == my_c)
    dx = ((group // 2) % 4 - my_x) % 4
    unit_of = (jnp.arange(16)[:, None] * BLOCKS + a)[:, :, None]
    block = jnp.where(mine, dx * BLOCKS + b % BLOCKS, -1)
    unit_of = jnp.max(jnp.where(block[:, :, None] == jnp.arange(16), unit_of + 1, 0), axis=1).T.reshape(256)
    listed = (unit_of > 0).reshape(16, 16)
    order = jnp.arange(16)
    rank = jnp.sum(listed[:, None, :] & (order[None, None, :] < order[None, :, None]), axis=2)
    steps = (jnp.sum(listed, axis=1) + 1) // 2
    first = jnp.sum(jnp.where(order[None, :] < jnp.arange(17)[:, None], steps[None, :], 0), axis=1)
    at = jnp.where(listed, 2 * first[:16, None] + rank, -1).reshape(256)
    todo = jnp.max(jnp.where(at == jnp.arange(80)[:, None], unit_of, 0), axis=1)
    todo = jnp.where(todo > 0, todo - 1, 64)
    left_tags = jnp.pad(left_tags, ((0, 8), (0, 0)), constant_values=-3.0)

    operands, known, right_at, meta_at = [], {}, [], []

    def place_of(value):
        if id(value) not in known:
            known[id(value)] = len(operands)
            operands.append(value)
        return known[id(value)]

    for k in [(dx, dy) for dx in range(4) for dy in range(4)]:
        right_at.append([(place_of(value), base) for value, base in parts[k]])
        meta_at.append((place_of(metas[k][0]), metas[k][1]))
    left_best, right_best = pair_maxima(todo, first, place, left_tags, left_rows, operands, right_at, meta_at)
    from_left = lax.all_to_all(left_best.reshape(16, BLOCKS, ROWS), ("z", "c"), 0, 0, tiled=True)
    from_right = lax.all_to_all(right_best.reshape(16, BLOCKS, ROWS), ("x", "y"), 0, 0, tiled=True)
    return jnp.maximum(jnp.max(from_left, axis=0), jnp.max(from_right, axis=0))


def solution(mesh):
    wide = Mesh(mesh.devices.reshape(8, 4, 2, 4), ("z", "x", "c", "y"))
    dp = ("z", "x", "c")
    placed = (P(dp, "y", None), P(dp, "y"), P(dp, "y"), P(dp), P(dp))
    return jax.shard_map(local, mesh=wide, in_specs=placed, out_specs=P(dp, "y"), check_vma=False)
```

```python
import jax
import jax.numpy as jnp
from jax import lax
from jax.experimental import pallas as pl
from jax.experimental.pallas import tpu as pltpu
from jax.sharding import Mesh, PartitionSpec as P

epsilon = 1e-06
ROWS = 128
BLOCKS = 4
META = 16
HALF1 = 2 * ROWS + META
HALF2 = 2 * ROWS
FULL = HALF1 + HALF2
SLOTS = 8
DEPTH = 5
VMEM_LIMIT = 32 * 1024 * 1024


def unit_kernel(emb_ref, unit_ref):
    for block in range(BLOCKS):
        rows = emb_ref[block].astype(jnp.float32)
        scale = lax.rsqrt(jnp.sum(rows * rows, axis=-1, keepdims=True) + epsilon)
        unit_ref[block * ROWS : (block + 1) * ROWS, :] = (rows * scale).astype(jnp.bfloat16)


def message_kernel(unit_ref, meta_ref, full_ref):
    full_ref[: 2 * ROWS, :] = unit_ref[: 2 * ROWS, :]
    full_ref[2 * ROWS : HALF1, :] = meta_ref[...]
    full_ref[HALF1:, :] = unit_ref[2 * ROWS :, :]


def pair_kernel(right_at, meta_at, todo, first, place, left_tags, left_ref, *rest):
    refs = rest[:-13]
    left_out, *right_out = rest[-13:-8]
    left_buf, right_buf, right_meta, tags_buf, best_buf, left_best, left_sems, right_sems = rest[-8:]

    def fetch_right(j):
        for dy in range(4):
            ref, base = right_at[j // 4 * 4 + dy][j % 4]
            pltpu.make_async_copy(
                refs[ref].at[pl.ds(base, ROWS), :], right_buf.at[j, pl.ds(dy * ROWS, ROWS), :], right_sems.at[j]
            ).start()

    for k in range(16):
        ref, row = meta_at[k]
        pltpu.make_async_copy(refs[ref].at[pl.ds(row, META), :], right_meta.at[k], right_sems.at[16]).start()
    for j in range(4):
        fetch_right(j)

    count = first[16]

    def each_left(i, act):
        slot = lax.rem(i, SLOTS)
        for h in range(2):
            unit = todo[2 * i + h]
            into = left_buf.at[slot, pl.ds(h * ROWS, ROWS), :]

            @pl.when(unit < 64)
            def _():
                row = pl.multiple_of(unit * ROWS, ROWS)
                act(pltpu.make_async_copy(left_ref.at[pl.ds(row, ROWS), :], into, left_sems.at[slot, h]))

    def fetch_left(i):
        each_left(i, lambda copy: copy.start())

    def early(i, carry):
        fetch_left(i)
        return carry

    lax.fori_loop(0, jnp.minimum(count, SLOTS), early, 0)
    for j in range(4, 16):
        fetch_right(j)
    left_best[...] = jnp.full(left_best.shape, -1.0, jnp.float32)
    pltpu.make_async_copy(right_meta, right_meta, right_sems.at[16]).wait()

    row_ids = lax.broadcasted_iota(jnp.int32, (ROWS, ROWS), 0)
    col_ids = lax.broadcasted_iota(jnp.int32, (ROWS, ROWS), 1)
    me = place[0]

    for j in range(16):
        dx, b = j // 4, j % 4
        for dy in range(4):
            row = right_meta[dx * 4 + dy, 0:1, b * ROWS : (b + 1) * ROWS].astype(jnp.float32)
            row = jnp.where(row < 0.0, -2.0, row)
            tags_buf[dy * ROWS : (dy + 1) * ROWS, :] = jnp.broadcast_to(row, (ROWS, ROWS)).T
        best_buf[...] = jnp.full(best_buf.shape, -1.0, jnp.float32)
        pltpu.make_async_copy(right_buf.at[j], right_buf.at[j], right_sems.at[j]).wait()

        def step(i, carry):
            each_left(i, lambda copy: copy.wait())
            scores = lax.dot_general(
                right_buf[j], left_buf[lax.rem(i, SLOTS)], (((1,), (1,)), ((), ())), preferred_element_type=jnp.float32
            )
            for h in range(2):
                unit = todo[2 * i + h]
                tags = left_tags[pl.ds(unit, 1), :]
                top = None
                for dy in range(4):
                    part = slice(dy * ROWS, (dy + 1) * ROWS)
                    keep = tags_buf[part, :] == tags
                    if dx == 0 and dy == 0:
                        keep = keep & ((row_ids != col_ids) | (unit != me * 4 + b))
                    masked = jnp.where(keep, scores[part, h * ROWS : (h + 1) * ROWS], -1.0)
                    best_buf[part, :] = jnp.maximum(best_buf[part, :], masked)
                    top = masked if top is None else jnp.maximum(top, masked)
                top = jnp.max(top, axis=0, keepdims=True)
                left_best[pl.ds(unit, 1), :] = jnp.maximum(left_best[pl.ds(unit, 1), :], top)

            @pl.when(i + SLOTS < count)
            def _():
                fetch_left(i + SLOTS)

            return carry

        lax.fori_loop(first[j], first[j + 1], step, 0)
        for dy in range(4):
            right_out[dy][j : j + 1, :] = jnp.max(best_buf[dy * ROWS : (dy + 1) * ROWS, :].T, axis=0, keepdims=True)
    left_out[...] = left_best[0:64, :]


def pair_maxima(todo, first, place, left_tags, left_rows, operands, right_at, meta_at):
    def kernel(*refs):
        pair_kernel(right_at, meta_at, *refs)

    smem, vmem, hbm = (pl.BlockSpec(memory_space=s) for s in (pltpu.SMEM, pltpu.VMEM, pltpu.HBM))
    return pl.pallas_call(
        kernel,
        out_shape=[jax.ShapeDtypeStruct((n, ROWS), jnp.float32) for n in (64, 16, 16, 16, 16)],
        in_specs=[smem, smem, smem, vmem] + [hbm] * (len(operands) + 1),
        out_specs=[vmem] * 5,
        scratch_shapes=[
            pltpu.VMEM((SLOTS, 2 * ROWS, 1024), jnp.bfloat16),
            pltpu.VMEM((16, 4 * ROWS, 1024), jnp.bfloat16),
            pltpu.VMEM((16, META, 1024), jnp.bfloat16),
            pltpu.VMEM((4 * ROWS, ROWS), jnp.float32),
            pltpu.VMEM((4 * ROWS, ROWS), jnp.float32),
            pltpu.VMEM((72, ROWS), jnp.float32),
            pltpu.SemaphoreType.DMA((SLOTS, 2)),
            pltpu.SemaphoreType.DMA((17,)),
        ],
        compiler_params=pltpu.CompilerParams(vmem_limit_bytes=VMEM_LIMIT),
        name="pair_maxima",
    )(todo, first, place, left_tags, *(pltpu.with_memory_space_constraint(v, pltpu.HBM) for v in (left_rows, *operands)))


def shift(value, axis, by):
    size = lax.axis_size(axis)
    return lax.ppermute(value, axis, [((i + by) % size, i) for i in range(size)])


class Carrier:
    def __init__(self):
        self.last = {}

    def __call__(self, value, axis, by):
        if (axis, by) in self.last:
            before = self.last[axis, by]
            value, before[0] = lax.optimization_barrier((value, before[0]))
        self.last[axis, by] = cell = [shift(value, axis, by)]
        return cell


def gather_plane(own, extra):
    send = Carrier()
    xp, xm, yp, ym = ("x", 1), ("x", -1), ("y", 1), ("y", -1)
    whole = {(0, 0): [own]}
    whole[0, 1], whole[0, 3] = send(own, *yp), send(own, *ym)
    whole[1, 0], whole[3, 0] = send(own, *xp), send(own, *xm)
    whole[0, 1][0], extra = lax.optimization_barrier((whole[0, 1][0], extra))
    whole[1, 1] = send(whole[0, 1][0], *xp)
    whole[3, 3] = send(whole[0, 3][0], *xm)
    whole[3, 1] = send(whole[3, 0][0], *yp)
    whole[1, 3] = send(whole[1, 0][0], *ym)
    whole[1, 2] = send(whole[1, 1][0], *yp)
    whole[3, 2] = send(whole[3, 3][0], *ym)
    whole[2, 3] = send(whole[1, 3][0], *xp)
    whole[2, 1] = send(whole[3, 1][0], *xm)
    half = {}
    half["y", 0] = send(whole[0, 1][0][:HALF1], *yp)
    half["y", 1] = send(whole[0, 3][0][HALF1:], *ym)
    half["x", 0] = send(whole[1, 0][0][:HALF1], *xp)
    half["x", 1] = send(whole[3, 0][0][HALF1:], *xm)
    last = [
        send(whole[1, 2][0][:ROWS], *xp),
        send(whole[3, 2][0][ROWS:HALF1], *xm),
        send(whole[2, 3][0][HALF1 : HALF1 + ROWS], *ym),
        send(whole[2, 1][0][HALF1 + ROWS :], *yp),
    ]
    starts = (0, ROWS, HALF1, HALF1 + ROWS)
    parts = {key: [(v[0], at) for at in starts] for key, v in whole.items()}
    metas = {key: (v[0], 2 * ROWS) for key, v in whole.items()}
    for key, axis in (((2, 0), "x"), ((0, 2), "y")):
        h1, h2 = half[axis, 0][0], half[axis, 1][0]
        parts[key] = [(h1, 0), (h1, ROWS), (h2, 0), (h2, ROWS)]
        metas[key] = (h1, 2 * ROWS)
    parts[2, 2] = [(v[0], 0) for v in last]
    metas[2, 2] = (last[1][0], ROWS)
    return parts, metas, extra


def local(embeddings, cluster_ids, valid, pair_left, pair_right):
    my_z, my_x, my_c = (lax.axis_index(name) for name in ("z", "x", "c"))
    place = (my_z * 2 + my_c).astype(jnp.int32).reshape(1)
    limit = pltpu.CompilerParams(vmem_limit_bytes=VMEM_LIMIT)
    unit = pl.pallas_call(
        unit_kernel, out_shape=jax.ShapeDtypeStruct((4 * ROWS, 1024), jnp.bfloat16), compiler_params=limit, name="unit_rows"
    )(embeddings)
    unit, cluster_ids, pair_left = lax.optimization_barrier((unit, cluster_ids, pair_left))
    left_rows = lax.all_gather(unit, ("z", "c"), axis=0, tiled=True)
    labels = jnp.where(valid > 0, cluster_ids, -1).reshape(1, -1)
    lists = jnp.concatenate([labels, (pair_left % BLOCKS)[None], pair_right[None]], axis=1)
    meta = jnp.pad(lists.astype(jnp.bfloat16), ((0, META - 1), (0, 1024 - lists.shape[1])))
    full = pl.pallas_call(
        message_kernel, out_shape=jax.ShapeDtypeStruct((FULL, 1024), jnp.bfloat16), compiler_params=limit, name="message_rows"
    )(unit, meta)
    full, lists = lax.optimization_barrier((full, lists))
    left_lists = lax.all_to_all(jnp.broadcast_to(lists, (16, lists.shape[1])), ("z", "c"), 0, 0, tiled=True)
    parts, metas, left_lists = gather_plane(full, left_lists)

    left_tags = left_lists[:, :512].astype(jnp.float32).reshape(64, ROWS)
    a, b = left_lists[:, 512:544], left_lists[:, 544:]
    group = b // BLOCKS
    mine = (group // 8 == my_z) & (group % 2 == my_c)
    dx = ((group // 2) % 4 - my_x) % 4
    unit_of = (jnp.arange(16)[:, None] * BLOCKS + a)[:, :, None]
    block = jnp.where(mine, dx * BLOCKS + b % BLOCKS, -1)
    unit_of = jnp.max(jnp.where(block[:, :, None] == jnp.arange(16), unit_of + 1, 0), axis=1).T.reshape(256)
    listed = (unit_of > 0).reshape(16, 16)
    order = jnp.arange(16)
    rank = jnp.sum(listed[:, None, :] & (order[None, None, :] < order[None, :, None]), axis=2)
    steps = (jnp.sum(listed, axis=1) + 1) // 2
    first = jnp.sum(jnp.where(order[None, :] < jnp.arange(17)[:, None], steps[None, :], 0), axis=1)
    at = jnp.where(listed, 2 * first[:16, None] + rank, -1).reshape(256)
    todo = jnp.max(jnp.where(at == jnp.arange(80)[:, None], unit_of, 0), axis=1)
    todo = jnp.where(todo > 0, todo - 1, 64)
    left_tags = jnp.pad(left_tags, ((0, 8), (0, 0)), constant_values=-3.0)

    operands, known, right_at, meta_at = [], {}, [], []

    def place_of(value):
        if id(value) not in known:
            known[id(value)] = len(operands)
            operands.append(value)
        return known[id(value)]

    for k in [(dx, dy) for dx in range(4) for dy in range(4)]:
        right_at.append([(place_of(value), base) for value, base in parts[k]])
        meta_at.append((place_of(metas[k][0]), metas[k][1]))
    left_best, *right_best = pair_maxima(todo, first, place, left_tags, left_rows, operands, right_at, meta_at)
    from_left = lax.all_to_all(left_best.reshape(16, BLOCKS, ROWS), ("z", "c"), 0, 0, tiled=True)
    own = right_best[0]
    for came in [shift(right_best[dy], "y", -dy) for dy in (1, 2, 3)]:
        own = jnp.maximum(own, came)
    best = own[:BLOCKS]
    for came in [shift(own[dx * BLOCKS : (dx + 1) * BLOCKS], "x", -dx) for dx in (1, 2, 3)]:
        best = jnp.maximum(best, came)
    return jnp.maximum(jnp.max(from_left, axis=0), best)


def solution(mesh):
    wide = Mesh(mesh.devices.reshape(8, 4, 2, 4), ("z", "x", "c", "y"))
    dp = ("z", "x", "c")
    placed = (P(dp, "y", None), P(dp, "y"), P(dp, "y"), P(dp), P(dp))
    return jax.shard_map(local, mesh=wide, in_specs=placed, out_specs=P(dp, "y"), check_vma=False)
```

```python
import jax
import jax.numpy as jnp
from jax import lax
from jax.experimental import pallas as pl
from jax.experimental.pallas import tpu as pltpu
from jax.sharding import Mesh, PartitionSpec as P

epsilon = 1e-06
ROWS = 128
BLOCKS = 4
META = 16
HALF1 = 2 * ROWS + META
HALF2 = 2 * ROWS
FULL = HALF1 + HALF2
SLOTS = 8
DEPTH = 5
VMEM_LIMIT = 32 * 1024 * 1024


def unit_kernel(emb_ref, unit_ref):
    for block in range(BLOCKS):
        rows = emb_ref[block].astype(jnp.float32)
        scale = lax.rsqrt(jnp.sum(rows * rows, axis=-1, keepdims=True) + epsilon)
        unit_ref[block * ROWS : (block + 1) * ROWS, :] = (rows * scale).astype(jnp.bfloat16)


def message_kernel(unit_ref, meta_ref, full_ref):
    full_ref[: 2 * ROWS, :] = unit_ref[: 2 * ROWS, :]
    full_ref[2 * ROWS : HALF1, :] = meta_ref[...]
    full_ref[HALF1:, :] = unit_ref[2 * ROWS :, :]


def pair_kernel(right_at, meta_at, todo, block_of, used, place, left_tags, left_ref, *rest):
    refs = rest[:-15]
    left_out, *right_out = rest[-15:-10]
    left_buf, tags_buf, right_buf, right_meta, right_tags, even, odd, left_best, right_best, sems = rest[-10:]
    left_sems, right_sems = sems.at[0], sems.at[1]

    def each_right(j, act):
        for dy in range(4):
            ref, base = right_at[j // 4 * 4 + dy][j % 4]
            act(refs[ref].at[pl.ds(base, ROWS), :], right_buf.at[j, pl.ds(dy * ROWS, ROWS), :])

    def fetch_right(j):
        @pl.when(used[j] > 0)
        def _():
            each_right(j, lambda source, into: pltpu.make_async_copy(source, into, right_sems.at[j]).start())

    def each_left(i, act):
        slot = lax.rem(i, SLOTS)
        for h in range(2):
            unit = todo[2 * i + h]
            part = pl.ds(h * ROWS, ROWS)
            act(pltpu.make_async_copy(left_tags.at[unit], tags_buf.at[slot, part, :], left_sems.at[2 * SLOTS + slot * 2 + h]))

            @pl.when(unit < 64)
            def _():
                row = pl.multiple_of(unit * ROWS, ROWS)
                act(pltpu.make_async_copy(left_ref.at[pl.ds(row, ROWS), :], left_buf.at[slot, part, :], left_sems.at[slot * 2 + h]))

    count = used[16]
    for k in range(16):
        ref, row = meta_at[k]
        pltpu.make_async_copy(refs[ref].at[pl.ds(row, META), :], right_meta.at[k], right_sems.at[16]).start()
    for j in range(2):
        fetch_right(j)
    for i in range(SLOTS):

        @pl.when(i < count + 2)
        def _(i=i):
            each_left(jnp.int32(i), lambda copy: copy.start())

    for j in range(2, 16):
        fetch_right(j)
    left_best[...] = jnp.full(left_best.shape, -1.0, jnp.float32)
    right_best[...] = jnp.full(right_best.shape, -1.0, jnp.float32)
    pltpu.make_async_copy(right_meta, right_meta, right_sems.at[16]).wait()
    for k in range(16):
        row = right_meta[k, 0:1, : 4 * ROWS].astype(jnp.float32)
        row = jnp.where(row < 0.0, -2.0, row)
        for b in range(4):
            j = k // 4 * 4 + b
            right_tags[j : j + 1, k % 4 * ROWS : (k % 4 + 1) * ROWS] = row[:, b * ROWS : (b + 1) * ROWS]

    off_diagonal = lax.broadcasted_iota(jnp.int32, (ROWS, ROWS), 0) != lax.broadcasted_iota(jnp.int32, (ROWS, ROWS), 1)
    me = place[0]

    def arrive(i):
        each_left(i, lambda copy: copy.wait())
        j = block_of[i]
        before = block_of[jnp.maximum(i - 1, 0)]

        @pl.when((i < used[17]) & ((i == 0) | (j != before)))
        def _():
            pltpu.make_async_copy(right_buf.at[j], right_buf.at[j], right_sems.at[j]).wait()

    def multiply(i, into):
        into[...] = lax.dot_general(
            left_buf[lax.rem(i, SLOTS)], right_buf[block_of[i]], (((1,), (1,)), ((), ())), preferred_element_type=jnp.float32
        )

    def maxima(i, scores):
        slot, j = lax.rem(i, SLOTS), block_of[i]
        right_row = right_tags[pl.ds(j, 1), :]
        tops = [None] * 4
        for h in range(2):
            unit = todo[2 * i + h]
            tags = tags_buf[slot, h * ROWS : (h + 1) * ROWS, :]
            same = (j < 4) & (unit == me * 4 + j)
            best = None
            for dy in range(4):
                cols = slice(dy * ROWS, (dy + 1) * ROWS)
                keep = tags == right_row[:, cols]
                if dy == 0:
                    keep = keep & (off_diagonal | jnp.logical_not(same))
                masked = jnp.where(keep, scores[h * ROWS : (h + 1) * ROWS, cols], -1.0)
                best = masked if best is None else jnp.maximum(best, masked)
                top = jnp.max(masked, axis=0, keepdims=True)
                tops[dy] = top if tops[dy] is None else jnp.maximum(tops[dy], top)
            best = jnp.max(best.T, axis=0, keepdims=True)
            left_best[pl.ds(unit, 1), :] = jnp.maximum(left_best[pl.ds(unit, 1), :], best)
        right_best[pl.ds(j, 1), :] = jnp.maximum(right_best[pl.ds(j, 1), :], jnp.concatenate(tops, axis=1))

    def refill(i):
        @pl.when(i + SLOTS < count + 2)
        def _():
            each_left(i + SLOTS, lambda copy: copy.start())

    arrive(jnp.int32(0))
    multiply(jnp.int32(0), even)

    def two(q, carry):
        i = 2 * q
        arrive(i + 1)
        multiply(i + 1, odd)
        maxima(i, even)
        refill(i)
        arrive(i + 2)
        multiply(i + 2, even)
        maxima(i + 1, odd)
        refill(i + 1)
        return carry

    lax.fori_loop(0, count // 2, two, 0)
    each_left(count + 1, lambda copy: copy.wait())
    left_out[...] = left_best[0:64, :]
    for dy in range(4):
        right_out[dy][...] = right_best[:, dy * ROWS : (dy + 1) * ROWS]


def pair_maxima(todo, block_of, used, place, left_tags, left_rows, operands, right_at, meta_at):
    def kernel(*refs):
        pair_kernel(right_at, meta_at, *refs)

    smem, vmem, hbm = (pl.BlockSpec(memory_space=s) for s in (pltpu.SMEM, pltpu.VMEM, pltpu.HBM))
    return pl.pallas_call(
        kernel,
        out_shape=[jax.ShapeDtypeStruct((n, ROWS), jnp.float32) for n in (64, 16, 16, 16, 16)],
        in_specs=[smem] * 4 + [hbm] * (len(operands) + 2),
        out_specs=[vmem] * 5,
        scratch_shapes=[
            pltpu.VMEM((SLOTS, 2 * ROWS, 1024), jnp.bfloat16),
            pltpu.VMEM((SLOTS, 2 * ROWS, ROWS), jnp.float32),
            pltpu.VMEM((16, 4 * ROWS, 1024), jnp.bfloat16),
            pltpu.VMEM((16, META, 1024), jnp.bfloat16),
            pltpu.VMEM((16, 4 * ROWS), jnp.float32),
            pltpu.VMEM((2 * ROWS, 4 * ROWS), jnp.float32),
            pltpu.VMEM((2 * ROWS, 4 * ROWS), jnp.float32),
            pltpu.VMEM((72, ROWS), jnp.float32),
            pltpu.VMEM((16, 4 * ROWS), jnp.float32),
            pltpu.SemaphoreType.DMA((2, 4 * SLOTS)),
        ],
        compiler_params=pltpu.CompilerParams(vmem_limit_bytes=VMEM_LIMIT),
        name="pair_maxima",
    )(todo, block_of, used, place, *(pltpu.with_memory_space_constraint(v, pltpu.HBM) for v in (left_tags, left_rows, *operands)))


def shift(value, axis, by):
    size = lax.axis_size(axis)
    return lax.ppermute(value, axis, [((i + by) % size, i) for i in range(size)])


class Carrier:
    def __init__(self):
        self.last = {}

    def __call__(self, value, axis, by):
        if (axis, by) in self.last:
            before = self.last[axis, by]
            value, before[0] = lax.optimization_barrier((value, before[0]))
        self.last[axis, by] = cell = [shift(value, axis, by)]
        return cell


def gather_plane(own, extra):
    send = Carrier()
    xp, xm, yp, ym = ("x", 1), ("x", -1), ("y", 1), ("y", -1)
    whole = {(0, 0): [own]}
    whole[0, 1], whole[0, 3] = send(own, *yp), send(own, *ym)
    whole[1, 0], whole[3, 0] = send(own, *xp), send(own, *xm)
    whole[0, 1][0], extra = lax.optimization_barrier((whole[0, 1][0], extra))
    half = {}
    whole[1, 1], half["y", 0] = send(whole[0, 1][0], *xp), send(whole[0, 1][0][:HALF1], *yp)
    whole[3, 3], half["y", 1] = send(whole[0, 3][0], *xm), send(whole[0, 3][0][HALF1:], *ym)
    whole[3, 1], whole[1, 3] = send(whole[3, 0][0], *yp), send(whole[1, 0][0], *ym)
    half["x", 0], half["x", 1] = send(whole[1, 0][0][:HALF1], *xp), send(whole[3, 0][0][HALF1:], *xm)
    whole[1, 2], whole[3, 2] = send(whole[1, 1][0], *yp), send(whole[3, 3][0], *ym)
    whole[2, 3], whole[2, 1] = send(whole[1, 3][0], *xp), send(whole[3, 1][0], *xm)
    last = [
        send(whole[1, 2][0][:ROWS], *xp),
        send(whole[3, 2][0][ROWS:HALF1], *xm),
        send(whole[2, 3][0][HALF1 : HALF1 + ROWS], *ym),
        send(whole[2, 1][0][HALF1 + ROWS :], *yp),
    ]
    starts = (0, ROWS, HALF1, HALF1 + ROWS)
    parts = {key: [(v[0], at) for at in starts] for key, v in whole.items()}
    metas = {key: (v[0], 2 * ROWS) for key, v in whole.items()}
    for key, axis in (((2, 0), "x"), ((0, 2), "y")):
        h1, h2 = half[axis, 0][0], half[axis, 1][0]
        parts[key] = [(h1, 0), (h1, ROWS), (h2, 0), (h2, ROWS)]
        metas[key] = (h1, 2 * ROWS)
    parts[2, 2] = [(v[0], 0) for v in last]
    metas[2, 2] = (last[1][0], ROWS)
    return parts, metas, extra


def local(embeddings, cluster_ids, valid, pair_left, pair_right):
    my_z, my_x, my_c = (lax.axis_index(name) for name in ("z", "x", "c"))
    place = (my_z * 2 + my_c).astype(jnp.int32).reshape(1)
    limit = pltpu.CompilerParams(vmem_limit_bytes=VMEM_LIMIT)
    unit = pl.pallas_call(
        unit_kernel, out_shape=jax.ShapeDtypeStruct((4 * ROWS, 1024), jnp.bfloat16), compiler_params=limit, name="unit_rows"
    )(embeddings)
    unit, cluster_ids, pair_left = lax.optimization_barrier((unit, cluster_ids, pair_left))
    left_rows = lax.all_gather(unit, ("z", "c"), axis=0, tiled=True)
    labels = jnp.where(valid > 0, cluster_ids, -1).reshape(1, -1)
    lists = jnp.concatenate([labels, (pair_left % BLOCKS)[None], pair_right[None]], axis=1)
    meta = jnp.pad(lists.astype(jnp.bfloat16), ((0, META - 1), (0, 1024 - lists.shape[1])))
    full = pl.pallas_call(
        message_kernel, out_shape=jax.ShapeDtypeStruct((FULL, 1024), jnp.bfloat16), compiler_params=limit, name="message_rows"
    )(unit, meta)
    full, lists = lax.optimization_barrier((full, lists))
    left_lists = lax.all_to_all(jnp.broadcast_to(lists, (16, lists.shape[1])), ("z", "c"), 0, 0, tiled=True)
    parts, metas, left_lists = gather_plane(full, left_lists)

    left_tags = left_lists[:, :512].astype(jnp.float32).reshape(64, ROWS)
    a, b = left_lists[:, 512:544], left_lists[:, 544:]
    group = b // BLOCKS
    mine = (group // 8 == my_z) & (group % 2 == my_c)
    dx = ((group // 2) % 4 - my_x) % 4
    unit_of = (jnp.arange(16)[:, None] * BLOCKS + a)[:, :, None]
    block = jnp.where(mine, dx * BLOCKS + b % BLOCKS, -1)
    unit_of = jnp.max(jnp.where(block[:, :, None] == jnp.arange(16), unit_of + 1, 0), axis=1).T.reshape(256)
    listed = (unit_of > 0).reshape(16, 16)
    order = jnp.arange(16)
    rank = jnp.sum(listed[:, None, :] & (order[None, None, :] < order[None, :, None]), axis=2)
    steps = (jnp.sum(listed, axis=1) + 1) // 2
    first = jnp.sum(jnp.where(order[None, :] < jnp.arange(17)[:, None], steps[None, :], 0), axis=1)
    at = jnp.where(listed, 2 * first[:16, None] + rank, -1).reshape(256)
    todo = jnp.max(jnp.where(at == jnp.arange(88)[:, None], unit_of, 0), axis=1)
    todo = jnp.where(todo > 0, todo - 1, 64)
    block_of = jnp.minimum(jnp.sum(first[None, 1:] <= jnp.arange(44)[:, None], axis=1), 15)
    used = jnp.concatenate([steps, (first[16:] + 1) // 2 * 2, first[16:]])
    left_tags = jnp.pad(left_tags, ((0, 1), (0, 0)), constant_values=-3.0)
    left_tags = jnp.broadcast_to(left_tags[:, :, None], (65, ROWS, ROWS))

    operands, known, right_at, meta_at = [], {}, [], []

    def place_of(value):
        if id(value) not in known:
            known[id(value)] = len(operands)
            operands.append(value)
        return known[id(value)]

    for k in [(dx, dy) for dx in range(4) for dy in range(4)]:
        right_at.append([(place_of(value), base) for value, base in parts[k]])
        meta_at.append((place_of(metas[k][0]), metas[k][1]))
    left_best, *right_best = pair_maxima(todo, block_of, used, place, left_tags, left_rows, operands, right_at, meta_at)
    from_left = lax.all_to_all(left_best.reshape(16, BLOCKS, ROWS), ("z", "c"), 0, 0, tiled=True)
    own = right_best[0]
    for came in [shift(right_best[dy], "y", -dy) for dy in (1, 2, 3)]:
        own = jnp.maximum(own, came)
    best = own[:BLOCKS]
    for came in [shift(own[dx * BLOCKS : (dx + 1) * BLOCKS], "x", -dx) for dx in (1, 2, 3)]:
        best = jnp.maximum(best, came)
    return jnp.maximum(jnp.max(from_left, axis=0), best)


def solution(mesh):
    wide = Mesh(mesh.devices.reshape(8, 4, 2, 4), ("z", "x", "c", "y"))
    dp = ("z", "x", "c")
    placed = (P(dp, "y", None), P(dp, "y"), P(dp, "y"), P(dp), P(dp))
    return jax.shard_map(local, mesh=wide, in_specs=placed, out_specs=P(dp, "y"), check_vma=False)
```

```python
import jax
import jax.numpy as jnp
from jax import lax
from jax.experimental import pallas as pl
from jax.experimental.pallas import tpu as pltpu
from jax.sharding import Mesh, PartitionSpec as P

epsilon = 1e-06
ROWS = 128
BLOCKS = 4
META = 16
HALF1 = 2 * ROWS + META
HALF2 = 2 * ROWS
FULL = HALF1 + HALF2
SLOTS = 8
DEPTH = 5
VMEM_LIMIT = 32 * 1024 * 1024


def unit_kernel(emb_ref, unit_ref):
    for block in range(BLOCKS):
        rows = emb_ref[block].astype(jnp.float32)
        scale = lax.rsqrt(jnp.sum(rows * rows, axis=-1, keepdims=True) + epsilon)
        unit_ref[block * ROWS : (block + 1) * ROWS, :] = (rows * scale).astype(jnp.bfloat16)


def message_kernel(unit_ref, meta_ref, full_ref):
    full_ref[: 2 * ROWS, :] = unit_ref[: 2 * ROWS, :]
    full_ref[2 * ROWS : HALF1, :] = meta_ref[...]
    full_ref[HALF1:, :] = unit_ref[2 * ROWS :, :]


def pair_kernel(right_at, meta_at, todo, block_of, used, place, left_tags, left_ref, *rest):
    refs = rest[:-15]
    left_out, *right_out = rest[-15:-10]
    left_buf, tags_buf, right_buf, right_meta, right_tags, even, odd, left_best, right_best, sems = rest[-10:]
    left_sems, right_sems = sems.at[0], sems.at[1]

    def each_right(j, act):
        for dy in range(4):
            ref, base = right_at[j // 4 * 4 + dy][j % 4]
            act(refs[ref].at[pl.ds(base, ROWS), :], right_buf.at[j, pl.ds(dy * ROWS, ROWS), :])

    def fetch_right(j):
        @pl.when(used[j] > 0)
        def _():
            each_right(j, lambda source, into: pltpu.make_async_copy(source, into, right_sems.at[j]).start())

    def each_left(i, act):
        slot = lax.rem(i, SLOTS)
        for h in range(2):
            unit = todo[2 * i + h]
            part = pl.ds(h * ROWS, ROWS)
            act(pltpu.make_async_copy(left_tags.at[unit], tags_buf.at[slot, part, :], left_sems.at[2 * SLOTS + slot * 2 + h]))

            @pl.when(unit < 64)
            def _():
                row = pl.multiple_of(unit * ROWS, ROWS)
                act(pltpu.make_async_copy(left_ref.at[pl.ds(row, ROWS), :], left_buf.at[slot, part, :], left_sems.at[slot * 2 + h]))

    count = used[16]
    for k in range(16):
        ref, row = meta_at[k]
        pltpu.make_async_copy(refs[ref].at[pl.ds(row, META), :], right_meta.at[k], right_sems.at[16]).start()
    for j in range(2):
        fetch_right(j)
    for i in range(SLOTS):

        @pl.when(i < count + 2)
        def _(i=i):
            each_left(jnp.int32(i), lambda copy: copy.start())

    for j in range(2, 16):
        fetch_right(j)
    left_best[...] = jnp.full(left_best.shape, -1.0, jnp.float32)
    right_best[...] = jnp.full(right_best.shape, -1.0, jnp.float32)
    pltpu.make_async_copy(right_meta, right_meta, right_sems.at[16]).wait()
    for k in range(16):
        row = right_meta[k, 0:1, : 4 * ROWS].astype(jnp.float32)
        row = jnp.where(row < 0.0, -2.0, row)
        for b in range(4):
            j = k // 4 * 4 + b
            right_tags[j : j + 1, k % 4 * ROWS : (k % 4 + 1) * ROWS] = row[:, b * ROWS : (b + 1) * ROWS]

    off_diagonal = lax.broadcasted_iota(jnp.int32, (ROWS, ROWS), 0) != lax.broadcasted_iota(jnp.int32, (ROWS, ROWS), 1)
    me = place[0]

    def arrive(i):
        each_left(i, lambda copy: copy.wait())
        j = block_of[i]
        before = block_of[jnp.maximum(i - 1, 0)]

        @pl.when((i < used[17]) & ((i == 0) | (j != before)))
        def _():
            pltpu.make_async_copy(right_buf.at[j], right_buf.at[j], right_sems.at[j]).wait()

    def multiply(i, into):
        into[...] = lax.dot_general(
            left_buf[lax.rem(i, SLOTS)], right_buf[block_of[i]], (((1,), (1,)), ((), ())), preferred_element_type=jnp.float32
        )

    def maxima(i, scores):
        slot, j = lax.rem(i, SLOTS), block_of[i]
        right_row = right_tags[pl.ds(j, 1), :]
        tops = [None] * 4
        for h in range(2):
            unit = todo[2 * i + h]
            tags = tags_buf[slot, h * ROWS : (h + 1) * ROWS, :]
            same = (j < 4) & (unit == me * 4 + j)
            best = None
            for dy in range(4):
                cols = slice(dy * ROWS, (dy + 1) * ROWS)
                keep = tags == right_row[:, cols]
                if dy == 0:
                    keep = keep & (off_diagonal | jnp.logical_not(same))
                masked = jnp.where(keep, scores[h * ROWS : (h + 1) * ROWS, cols], -1.0)
                best = masked if best is None else jnp.maximum(best, masked)
                top = jnp.max(masked, axis=0, keepdims=True)
                tops[dy] = top if tops[dy] is None else jnp.maximum(tops[dy], top)
            best = jnp.max(best.T, axis=0, keepdims=True)
            left_best[pl.ds(unit, 1), :] = jnp.maximum(left_best[pl.ds(unit, 1), :], best)
        right_best[pl.ds(j, 1), :] = jnp.maximum(right_best[pl.ds(j, 1), :], jnp.concatenate(tops, axis=1))

    def refill(i):
        @pl.when(i + SLOTS < count + 2)
        def _():
            each_left(i + SLOTS, lambda copy: copy.start())

    arrive(jnp.int32(0))
    multiply(jnp.int32(0), even)

    def two(q, carry):
        i = 2 * q
        arrive(i + 1)
        multiply(i + 1, odd)
        maxima(i, even)
        refill(i)
        arrive(i + 2)
        multiply(i + 2, even)
        maxima(i + 1, odd)
        refill(i + 1)
        return carry

    lax.fori_loop(0, count // 2, two, 0)
    each_left(count + 1, lambda copy: copy.wait())
    left_out[...] = left_best[0:64, :]
    for dy in range(4):
        right_out[dy][...] = right_best[:, dy * ROWS : (dy + 1) * ROWS]


def pair_maxima(todo, block_of, used, place, left_tags, left_rows, operands, right_at, meta_at):
    def kernel(*refs):
        pair_kernel(right_at, meta_at, *refs)

    smem, vmem, hbm = (pl.BlockSpec(memory_space=s) for s in (pltpu.SMEM, pltpu.VMEM, pltpu.HBM))
    return pl.pallas_call(
        kernel,
        out_shape=[jax.ShapeDtypeStruct((n, ROWS), jnp.float32) for n in (64, 16, 16, 16, 16)],
        in_specs=[smem] * 4 + [hbm] * (len(operands) + 2),
        out_specs=[vmem] * 5,
        scratch_shapes=[
            pltpu.VMEM((SLOTS, 2 * ROWS, 1024), jnp.bfloat16),
            pltpu.VMEM((SLOTS, 2 * ROWS, ROWS), jnp.float32),
            pltpu.VMEM((16, 4 * ROWS, 1024), jnp.bfloat16),
            pltpu.VMEM((16, META, 1024), jnp.bfloat16),
            pltpu.VMEM((16, 4 * ROWS), jnp.float32),
            pltpu.VMEM((2 * ROWS, 4 * ROWS), jnp.float32),
            pltpu.VMEM((2 * ROWS, 4 * ROWS), jnp.float32),
            pltpu.VMEM((72, ROWS), jnp.float32),
            pltpu.VMEM((16, 4 * ROWS), jnp.float32),
            pltpu.SemaphoreType.DMA((2, 4 * SLOTS)),
        ],
        compiler_params=pltpu.CompilerParams(vmem_limit_bytes=VMEM_LIMIT),
        name="pair_maxima",
    )(todo, block_of, used, place, *(pltpu.with_memory_space_constraint(v, pltpu.HBM) for v in (left_tags, left_rows, *operands)))


def shift(value, axis, by):
    size = lax.axis_size(axis)
    return lax.ppermute(value, axis, [((i + by) % size, i) for i in range(size)])


class Carrier:
    def __init__(self):
        self.last = {}

    def __call__(self, value, axis, by):
        if (axis, by) in self.last:
            before = self.last[axis, by]
            value, before[0] = lax.optimization_barrier((value, before[0]))
        self.last[axis, by] = cell = [shift(value, axis, by)]
        return cell


def gather_plane(own, extra, make_beside):
    send = Carrier()
    xp, xm, yp, ym = ("x", 1), ("x", -1), ("y", 1), ("y", -1)
    whole = {(0, 0): [own]}
    whole[0, 1], whole[0, 3] = send(own, *yp), send(own, *ym)
    whole[1, 0], whole[3, 0] = send(own, *xp), send(own, *xm)
    whole[0, 1][0], extra = lax.optimization_barrier((whole[0, 1][0], extra))
    whole[1, 1], whole[3, 3] = send(whole[0, 1][0], *xp), send(whole[0, 3][0], *xm)
    whole[3, 1], whole[1, 3] = send(whole[3, 0][0], *yp), send(whole[1, 0][0], *ym)
    cut = [whole[1, 0][0][:HALF1], whole[3, 0][0][HALF1:], whole[0, 1][0][:HALF1], whole[0, 3][0][HALF1:]]
    cut, whole[1, 1][0], beside = lax.optimization_barrier((cut, whole[1, 1][0], make_beside(extra)))
    half = {("x", 0): send(cut[0], *xp), ("x", 1): send(cut[1], *xm)}
    whole[1, 2], whole[3, 2] = send(whole[1, 1][0], *yp), send(whole[3, 3][0], *ym)
    whole[2, 3], whole[2, 1] = send(whole[1, 3][0], *xp), send(whole[3, 1][0], *xm)
    half["y", 0], half["y", 1] = send(cut[2], *yp), send(cut[3], *ym)
    last = [
        send(whole[1, 2][0][:ROWS], *xp),
        send(whole[3, 2][0][ROWS:HALF1], *xm),
        send(whole[2, 3][0][HALF1 : HALF1 + ROWS], *ym),
        send(whole[2, 1][0][HALF1 + ROWS :], *yp),
    ]
    starts = (0, ROWS, HALF1, HALF1 + ROWS)
    parts = {key: [(v[0], at) for at in starts] for key, v in whole.items()}
    metas = {key: (v[0], 2 * ROWS) for key, v in whole.items()}
    for key, axis in (((2, 0), "x"), ((0, 2), "y")):
        h1, h2 = half[axis, 0][0], half[axis, 1][0]
        parts[key] = [(h1, 0), (h1, ROWS), (h2, 0), (h2, ROWS)]
        metas[key] = (h1, 2 * ROWS)
    parts[2, 2] = [(v[0], 0) for v in last]
    metas[2, 2] = (last[1][0], ROWS)
    return parts, metas, beside


def pair_lists(left_lists):
    my_z, my_x, my_c = (lax.axis_index(name) for name in ("z", "x", "c"))
    place = (my_z * 2 + my_c).astype(jnp.int32).reshape(1)
    left_tags = left_lists[:, :512].astype(jnp.float32).reshape(64, ROWS)
    a, b = left_lists[:, 512:544], left_lists[:, 544:]
    group = b // BLOCKS
    mine = (group // 8 == my_z) & (group % 2 == my_c)
    dx = ((group // 2) % 4 - my_x) % 4
    unit_of = (jnp.arange(16)[:, None] * BLOCKS + a)[:, :, None]
    block = jnp.where(mine, dx * BLOCKS + b % BLOCKS, -1)
    unit_of = jnp.max(jnp.where(block[:, :, None] == jnp.arange(16), unit_of + 1, 0), axis=1).T.reshape(256)
    listed = (unit_of > 0).reshape(16, 16)
    order = jnp.arange(16)
    rank = jnp.sum(listed[:, None, :] & (order[None, None, :] < order[None, :, None]), axis=2)
    steps = (jnp.sum(listed, axis=1) + 1) // 2
    first = jnp.sum(jnp.where(order[None, :] < jnp.arange(17)[:, None], steps[None, :], 0), axis=1)
    at = jnp.where(listed, 2 * first[:16, None] + rank, -1).reshape(256)
    todo = jnp.max(jnp.where(at == jnp.arange(88)[:, None], unit_of, 0), axis=1)
    todo = jnp.where(todo > 0, todo - 1, 64)
    block_of = jnp.minimum(jnp.sum(first[None, 1:] <= jnp.arange(44)[:, None], axis=1), 15)
    used = jnp.concatenate([steps, (first[16:] + 1) // 2 * 2, first[16:]])
    left_tags = jnp.pad(left_tags, ((0, 1), (0, 0)), constant_values=-3.0)
    left_tags = jnp.broadcast_to(left_tags[:, :, None], (65, ROWS, ROWS))
    return todo, block_of, used, place, left_tags


def local(embeddings, cluster_ids, valid, pair_left, pair_right):
    limit = pltpu.CompilerParams(vmem_limit_bytes=VMEM_LIMIT)
    unit = pl.pallas_call(
        unit_kernel, out_shape=jax.ShapeDtypeStruct((4 * ROWS, 1024), jnp.bfloat16), compiler_params=limit, name="unit_rows"
    )(embeddings)
    unit, cluster_ids, pair_left = lax.optimization_barrier((unit, cluster_ids, pair_left))
    left_rows = lax.all_gather(unit, ("z", "c"), axis=0, tiled=True)
    labels = jnp.where(valid > 0, cluster_ids, -1).reshape(1, -1)
    lists = jnp.concatenate([labels, (pair_left % BLOCKS)[None], pair_right[None]], axis=1)
    meta = jnp.pad(lists.astype(jnp.bfloat16), ((0, META - 1), (0, 1024 - lists.shape[1])))
    full = pl.pallas_call(
        message_kernel, out_shape=jax.ShapeDtypeStruct((FULL, 1024), jnp.bfloat16), compiler_params=limit, name="message_rows"
    )(unit, meta)
    full, lists = lax.optimization_barrier((full, lists))
    left_lists = lax.all_to_all(jnp.broadcast_to(lists, (16, lists.shape[1])), ("z", "c"), 0, 0, tiled=True)
    parts, metas, beside = gather_plane(full, left_lists, pair_lists)

    operands, known, right_at, meta_at = [], {}, [], []

    def place_of(value):
        if id(value) not in known:
            known[id(value)] = len(operands)
            operands.append(value)
        return known[id(value)]

    for k in [(dx, dy) for dx in range(4) for dy in range(4)]:
        right_at.append([(place_of(value), base) for value, base in parts[k]])
        meta_at.append((place_of(metas[k][0]), metas[k][1]))
    left_best, *right_best = pair_maxima(*beside, left_rows, operands, right_at, meta_at)
    from_left = lax.all_to_all(left_best.reshape(16, BLOCKS, ROWS), ("z", "c"), 0, 0, tiled=True)
    own = right_best[0]
    for came in [shift(right_best[dy], "y", -dy) for dy in (1, 2, 3)]:
        own = jnp.maximum(own, came)
    best = own[:BLOCKS]
    for came in [shift(own[dx * BLOCKS : (dx + 1) * BLOCKS], "x", -dx) for dx in (1, 2, 3)]:
        best = jnp.maximum(best, came)
    return jnp.maximum(jnp.max(from_left, axis=0), best)


def solution(mesh):
    wide = Mesh(mesh.devices.reshape(8, 4, 2, 4), ("z", "x", "c", "y"))
    dp = ("z", "x", "c")
    placed = (P(dp, "y", None), P(dp, "y"), P(dp, "y"), P(dp), P(dp))
    return jax.shard_map(local, mesh=wide, in_specs=placed, out_specs=P(dp, "y"), check_vma=False)
```

```python
import jax
import jax.numpy as jnp
from jax import lax
from jax.experimental import pallas as pl
from jax.experimental.pallas import tpu as pltpu
from jax.sharding import Mesh, PartitionSpec as P

epsilon = 1e-06
ROWS = 128
BLOCKS = 4
META = 16
HALF1 = 2 * ROWS + META
HALF2 = 2 * ROWS
FULL = HALF1 + HALF2
SLOTS = 8
DEPTH = 5
VMEM_LIMIT = 32 * 1024 * 1024


def unit_kernel(emb_ref, unit_ref):
    for block in range(BLOCKS):
        rows = emb_ref[block].astype(jnp.float32)
        scale = lax.rsqrt(jnp.sum(rows * rows, axis=-1, keepdims=True) + epsilon)
        unit_ref[block * ROWS : (block + 1) * ROWS, :] = (rows * scale).astype(jnp.bfloat16)


def message_kernel(unit_ref, meta_ref, full_ref):
    full_ref[: 2 * ROWS, :] = unit_ref[: 2 * ROWS, :]
    full_ref[2 * ROWS : HALF1, :] = meta_ref[...]
    full_ref[HALF1:, :] = unit_ref[2 * ROWS :, :]


def pair_kernel(right_at, meta_at, todo, block_of, used, place, left_tags, left_ref, *rest):
    refs = rest[:-14]
    left_out, *right_out = rest[-14:-9]
    left_buf, right_buf, right_meta, right_tags, even, odd, left_best, right_best, sems = rest[-9:]
    left_sems, right_sems = sems.at[0], sems.at[1]

    def each_right(j, act):
        for dy in range(4):
            ref, base = right_at[j // 4 * 4 + dy][j % 4]
            act(refs[ref].at[pl.ds(base, ROWS), :], right_buf.at[j, pl.ds(dy * ROWS, ROWS), :])

    def fetch_right(j):
        @pl.when(used[j] > 0)
        def _():
            each_right(j, lambda source, into: pltpu.make_async_copy(source, into, right_sems.at[j]).start())

    def each_left(i, act):
        slot = lax.rem(i, SLOTS)
        for h in range(2):
            unit = todo[2 * i + h]
            part = pl.ds(h * ROWS, ROWS)

            @pl.when(unit < 64)
            def _():
                row = pl.multiple_of(unit * ROWS, ROWS)
                act(pltpu.make_async_copy(left_ref.at[pl.ds(row, ROWS), :], left_buf.at[slot, part, :], left_sems.at[slot * 2 + h]))

    count = used[16]
    for k in range(16):
        ref, row = meta_at[k]
        pltpu.make_async_copy(refs[ref].at[pl.ds(row, META), :], right_meta.at[k], right_sems.at[16]).start()
    for j in range(2):
        fetch_right(j)
    for i in range(SLOTS):

        @pl.when(i < count + 2)
        def _(i=i):
            each_left(jnp.int32(i), lambda copy: copy.start())

    for j in range(2, 16):
        fetch_right(j)
    left_best[...] = jnp.full(left_best.shape, -1.0, jnp.float32)
    right_best[...] = jnp.full(right_best.shape, -1.0, jnp.float32)
    pltpu.make_async_copy(right_meta, right_meta, right_sems.at[16]).wait()
    for k in range(16):
        row = right_meta[k, 0:1, : 4 * ROWS].astype(jnp.float32)
        row = jnp.where(row < 0.0, -2.0, row)
        for b in range(4):
            j = k // 4 * 4 + b
            right_tags[j : j + 1, k % 4 * ROWS : (k % 4 + 1) * ROWS] = row[:, b * ROWS : (b + 1) * ROWS]

    off_diagonal = lax.broadcasted_iota(jnp.int32, (ROWS, ROWS), 0) != lax.broadcasted_iota(jnp.int32, (ROWS, ROWS), 1)
    me = place[0]

    def arrive(i):
        each_left(i, lambda copy: copy.wait())
        j = block_of[i]
        before = block_of[jnp.maximum(i - 1, 0)]

        @pl.when((i < used[17]) & ((i == 0) | (j != before)))
        def _():
            pltpu.make_async_copy(right_buf.at[j], right_buf.at[j], right_sems.at[j]).wait()

    def multiply(i, into):
        into[...] = lax.dot_general(
            left_buf[lax.rem(i, SLOTS)], right_buf[block_of[i]], (((1,), (1,)), ((), ())), preferred_element_type=jnp.float32
        )

    def maxima(i, scores):
        j = block_of[i]
        right_row = right_tags[pl.ds(j, 1), :]
        tops = [None] * 4
        for h in range(2):
            unit = todo[2 * i + h]
            tags = jnp.broadcast_to(left_tags[pl.ds(unit, 1), :], (ROWS, ROWS)).T
            same = (j < 4) & (unit == me * 4 + j)
            best = None
            for dy in range(4):
                cols = slice(dy * ROWS, (dy + 1) * ROWS)
                keep = tags == right_row[:, cols]
                if dy == 0:
                    keep = keep & (off_diagonal | jnp.logical_not(same))
                masked = jnp.where(keep, scores[h * ROWS : (h + 1) * ROWS, cols], -1.0)
                best = masked if best is None else jnp.maximum(best, masked)
                top = jnp.max(masked, axis=0, keepdims=True)
                tops[dy] = top if tops[dy] is None else jnp.maximum(tops[dy], top)
            best = jnp.max(best.T, axis=0, keepdims=True)
            left_best[pl.ds(unit, 1), :] = jnp.maximum(left_best[pl.ds(unit, 1), :], best)
        right_best[pl.ds(j, 1), :] = jnp.maximum(right_best[pl.ds(j, 1), :], jnp.concatenate(tops, axis=1))

    def refill(i):
        @pl.when(i + SLOTS < count + 2)
        def _():
            each_left(i + SLOTS, lambda copy: copy.start())

    arrive(jnp.int32(0))
    multiply(jnp.int32(0), even)

    def two(q, carry):
        i = 2 * q
        arrive(i + 1)
        multiply(i + 1, odd)
        maxima(i, even)
        refill(i)
        arrive(i + 2)
        multiply(i + 2, even)
        maxima(i + 1, odd)
        refill(i + 1)
        return carry

    lax.fori_loop(0, count // 2, two, 0)
    each_left(count + 1, lambda copy: copy.wait())
    left_out[...] = left_best[0:64, :]
    for dy in range(4):
        right_out[dy][...] = right_best[:, dy * ROWS : (dy + 1) * ROWS]


def pair_maxima(todo, block_of, used, place, left_tags, left_rows, operands, right_at, meta_at):
    def kernel(*refs):
        pair_kernel(right_at, meta_at, *refs)

    smem, vmem, hbm = (pl.BlockSpec(memory_space=s) for s in (pltpu.SMEM, pltpu.VMEM, pltpu.HBM))
    return pl.pallas_call(
        kernel,
        out_shape=[jax.ShapeDtypeStruct((n, ROWS), jnp.float32) for n in (64, 16, 16, 16, 16)],
        in_specs=[smem] * 4 + [vmem] + [hbm] * (len(operands) + 1),
        out_specs=[vmem] * 5,
        scratch_shapes=[
            pltpu.VMEM((SLOTS, 2 * ROWS, 1024), jnp.bfloat16),
            pltpu.VMEM((16, 4 * ROWS, 1024), jnp.bfloat16),
            pltpu.VMEM((16, META, 1024), jnp.bfloat16),
            pltpu.VMEM((16, 4 * ROWS), jnp.float32),
            pltpu.VMEM((2 * ROWS, 4 * ROWS), jnp.float32),
            pltpu.VMEM((2 * ROWS, 4 * ROWS), jnp.float32),
            pltpu.VMEM((72, ROWS), jnp.float32),
            pltpu.VMEM((16, 4 * ROWS), jnp.float32),
            pltpu.SemaphoreType.DMA((2, 2 * SLOTS + 1)),
        ],
        compiler_params=pltpu.CompilerParams(vmem_limit_bytes=VMEM_LIMIT),
        name="pair_maxima",
    )(todo, block_of, used, place, left_tags, *(pltpu.with_memory_space_constraint(v, pltpu.HBM) for v in (left_rows, *operands)))


def shift(value, axis, by):
    size = lax.axis_size(axis)
    return lax.ppermute(value, axis, [((i + by) % size, i) for i in range(size)])


LINKS = {"x-": ("x", -1), "y-": ("y", -1), "x+": ("x", 1), "y+": ("y", 1)}
CARRIED = {"c": {"x+": "y+", "x-": "y-", "y+": "x-", "y-": "x+"}, "d": {"y+": "x+", "y-": "x-", "x+": "y-", "x-": "y+"}}
QUARTERS = {"x+": ("dy+", 0), "x-": ("dy-", ROWS), "y-": ("dx+", HALF1), "y+": ("dx-", HALF1 + ROWS)}
STEPS = (
    ("cx-", "cy-", "cx+", "cy+", "=", "dy-", "dy+", "bx-", "bx+"),
    ("dx-", "dx+", "by-", "by+", "ey-", "ey+", "ex-", "ex+"),
)
AFTER = {"bx": "cx", "dx": "bx", "ex": "dx", "dy": "cy", "by": "dy"}


def gather_plane(own, extra, make_beside):
    cells, cut = {}, {}

    def send(name, value):
        before = AFTER.get(name[:2])
        if before:
            other = cells[before + name[2]]
            value, other[0] = lax.optimization_barrier((value, other[0]))
        cells[name] = [shift(value, *LINKS[name[1:]])]

    for link in LINKS:
        send("a" + link, own)
    for step in STEPS[0] + STEPS[1]:
        kind, link = step[0], step[1:]
        if kind == "=":
            extra, cells["ay+"][0] = lax.optimization_barrier((extra, cells["ay+"][0]))
            for other in LINKS:
                cut[other] = cells["a" + other][0][:HALF1] if other[1] == "+" else cells["a" + other][0][HALF1:]
            cut, cells["cx+"][0], beside = lax.optimization_barrier((cut, cells["cx+"][0], make_beside(extra)))
        elif kind in CARRIED:
            send(step, cells[{"c": "a", "d": "c"}[kind] + CARRIED[kind][link]][0])
        elif kind == "b":
            send(step, cut[link])
        else:
            name, at = QUARTERS[link]
            send(step, cells[name][0][at : HALF1 if link == "x-" else at + ROWS])
    whole = {(0, 0): [own]}
    names = ("ax+", "ax-", "ay+", "ay-", "cx+", "cx-", "cy+", "cy-", "dy+", "dy-", "dx+", "dx-")
    spots = [(1, 0), (3, 0), (0, 1), (0, 3), (1, 1), (3, 3), (3, 1), (1, 3), (1, 2), (3, 2), (2, 3), (2, 1)]
    whole.update((spot, cells[name]) for spot, name in zip(spots, names))
    starts = (0, ROWS, HALF1, HALF1 + ROWS)
    parts = {key: [(v[0], at) for at in starts] for key, v in whole.items()}
    metas = {key: (v[0], 2 * ROWS) for key, v in whole.items()}
    for key, axis in (((2, 0), "x"), ((0, 2), "y")):
        h1, h2 = cells["b" + axis + "+"][0], cells["b" + axis + "-"][0]
        parts[key] = [(h1, 0), (h1, ROWS), (h2, 0), (h2, ROWS)]
        metas[key] = (h1, 2 * ROWS)
    parts[2, 2] = [(cells[name][0], 0) for name in ("ex+", "ex-", "ey-", "ey+")]
    metas[2, 2] = (cells["ex-"][0], ROWS)
    return parts, metas, beside


def pair_lists(left_lists):
    my_z, my_x, my_c = (lax.axis_index(name) for name in ("z", "x", "c"))
    place = (my_z * 2 + my_c).astype(jnp.int32).reshape(1)
    left_tags = left_lists[:, :512].astype(jnp.float32).reshape(64, ROWS)
    a, b = left_lists[:, 512:544], left_lists[:, 544:]
    group = b // BLOCKS
    mine = (group // 8 == my_z) & (group % 2 == my_c)
    dx = ((group // 2) % 4 - my_x) % 4
    unit_of = (jnp.arange(16)[:, None] * BLOCKS + a)[:, :, None]
    block = jnp.where(mine, dx * BLOCKS + b % BLOCKS, -1)
    unit_of = jnp.max(jnp.where(block[:, :, None] == jnp.arange(16), unit_of + 1, 0), axis=1).T.reshape(256)
    listed = (unit_of > 0).reshape(16, 16)
    order = jnp.arange(16)
    rank = jnp.sum(listed[:, None, :] & (order[None, None, :] < order[None, :, None]), axis=2)
    steps = (jnp.sum(listed, axis=1) + 1) // 2
    first = jnp.sum(jnp.where(order[None, :] < jnp.arange(17)[:, None], steps[None, :], 0), axis=1)
    at = jnp.where(listed, 2 * first[:16, None] + rank, -1).reshape(256)
    todo = jnp.max(jnp.where(at == jnp.arange(88)[:, None], unit_of, 0), axis=1)
    todo = jnp.where(todo > 0, todo - 1, 64)
    block_of = jnp.minimum(jnp.sum(first[None, 1:] <= jnp.arange(44)[:, None], axis=1), 15)
    used = jnp.concatenate([steps, (first[16:] + 1) // 2 * 2, first[16:]])
    left_tags = jnp.pad(left_tags, ((0, 8), (0, 0)), constant_values=-3.0)
    return todo, block_of, used, place, left_tags


def local(embeddings, cluster_ids, valid, pair_left, pair_right):
    limit = pltpu.CompilerParams(vmem_limit_bytes=VMEM_LIMIT)
    unit = pl.pallas_call(
        unit_kernel, out_shape=jax.ShapeDtypeStruct((4 * ROWS, 1024), jnp.bfloat16), compiler_params=limit, name="unit_rows"
    )(embeddings)
    unit, cluster_ids, pair_left = lax.optimization_barrier((unit, cluster_ids, pair_left))
    left_rows = lax.all_gather(unit, ("z", "c"), axis=0, tiled=True)
    labels = jnp.where(valid > 0, cluster_ids, -1).reshape(1, -1)
    lists = jnp.concatenate([labels, (pair_left % BLOCKS)[None], pair_right[None]], axis=1)
    meta = jnp.pad(lists.astype(jnp.bfloat16), ((0, META - 1), (0, 1024 - lists.shape[1])))
    full = pl.pallas_call(
        message_kernel, out_shape=jax.ShapeDtypeStruct((FULL, 1024), jnp.bfloat16), compiler_params=limit, name="message_rows"
    )(unit, meta)
    full, lists = lax.optimization_barrier((full, lists))
    left_lists = lax.all_to_all(jnp.broadcast_to(lists, (16, lists.shape[1])), ("z", "c"), 0, 0, tiled=True)
    parts, metas, beside = gather_plane(full, left_lists, pair_lists)

    operands, known, right_at, meta_at = [], {}, [], []

    def place_of(value):
        if id(value) not in known:
            known[id(value)] = len(operands)
            operands.append(value)
        return known[id(value)]

    for k in [(dx, dy) for dx in range(4) for dy in range(4)]:
        right_at.append([(place_of(value), base) for value, base in parts[k]])
        meta_at.append((place_of(metas[k][0]), metas[k][1]))
    left_best, *right_best = pair_maxima(*beside, left_rows, operands, right_at, meta_at)
    from_left = lax.all_to_all(left_best.reshape(16, BLOCKS, ROWS), ("z", "c"), 0, 0, tiled=True)
    own = right_best[0]
    for came in [shift(right_best[dy], "y", -dy) for dy in (1, 2, 3)]:
        own = jnp.maximum(own, came)
    best = own[:BLOCKS]
    for came in [shift(own[dx * BLOCKS : (dx + 1) * BLOCKS], "x", -dx) for dx in (1, 2, 3)]:
        best = jnp.maximum(best, came)
    return jnp.maximum(jnp.max(from_left, axis=0), best)


def solution(mesh):
    wide = Mesh(mesh.devices.reshape(8, 4, 2, 4), ("z", "x", "c", "y"))
    dp = ("z", "x", "c")
    placed = (P(dp, "y", None), P(dp, "y"), P(dp, "y"), P(dp), P(dp))
    return jax.shard_map(local, mesh=wide, in_specs=placed, out_specs=P(dp, "y"), check_vma=False)
```

```python
import jax
import jax.numpy as jnp
from jax import lax
from jax.experimental import pallas as pl
from jax.experimental.pallas import tpu as pltpu
from jax.sharding import Mesh, PartitionSpec as P

epsilon = 1e-06
ROWS = 128
BLOCKS = 4
META = 16
HALF1 = 2 * ROWS + META
HALF2 = 2 * ROWS
FULL = HALF1 + HALF2
SLOTS = 8
DEPTH = 5
VMEM_LIMIT = 32 * 1024 * 1024
COLUMNS = ((0, 1, 3), (2,))


def unit_kernel(ids_ref, valid_ref, emb_ref, unit_ref, full_ref, rows_buf, sems):
    copies = [pltpu.make_async_copy(emb_ref.at[block], rows_buf.at[block], sems.at[block]) for block in range(BLOCKS)]
    for copy in copies:
        copy.start()
    labels = jnp.where(valid_ref[...] > 0, ids_ref[...], -1).astype(jnp.float32).astype(jnp.bfloat16)
    full_ref[2 * ROWS : HALF1, :] = jnp.zeros((META, 1024), jnp.bfloat16)
    for block in range(BLOCKS):
        full_ref[2 * ROWS : 2 * ROWS + 1, block * ROWS : (block + 1) * ROWS] = labels[block : block + 1, :]
        copies[block].wait()
        rows = rows_buf[block].astype(jnp.float32)
        scale = lax.rsqrt(jnp.sum(rows * rows, axis=-1, keepdims=True) + epsilon)
        unit = (rows * scale).astype(jnp.bfloat16)
        unit_ref[block * ROWS : (block + 1) * ROWS, :] = unit
        at = block * ROWS + (META if block >= 2 else 0)
        full_ref[at : at + ROWS, :] = unit


def pair_kernel(columns, right_at, meta_at, todo, block_of, used, place, left_tags, *rest):
    blocks = 4 * len(columns)
    before, left_ref, refs = rest[:5], rest[5], rest[6:-14]
    left_out, *right_out = rest[-14:-9]
    left_buf, right_buf, right_meta, right_tags, even, odd, left_best, right_best, sems = rest[-9:]
    left_sems, right_sems = sems.at[0], sems.at[1]

    def each_right(j, act):
        for dy in range(4):
            ref, base = right_at[columns[j // 4] * 4 + dy][j % 4]
            act(refs[ref].at[pl.ds(base, ROWS), :], right_buf.at[j, pl.ds(dy * ROWS, ROWS), :])

    def fetch_right(j):
        @pl.when(used[j] > 0)
        def _():
            each_right(j, lambda source, into: pltpu.make_async_copy(source, into, right_sems.at[j]).start())

    def each_left(i, act):
        slot = lax.rem(i, SLOTS)
        for h in range(2):
            unit = todo[2 * i + h]
            part = pl.ds(h * ROWS, ROWS)

            @pl.when(unit < 64)
            def _():
                row = pl.multiple_of(unit * ROWS, ROWS)
                act(pltpu.make_async_copy(left_ref.at[pl.ds(row, ROWS), :], left_buf.at[slot, part, :], left_sems.at[slot * 2 + h]))

    count = used[blocks]
    for k in range(blocks):
        ref, row = meta_at[columns[k // 4] * 4 + k % 4]
        pltpu.make_async_copy(refs[ref].at[pl.ds(row, META), :], right_meta.at[k], right_sems.at[blocks]).start()
    for j in range(2):
        fetch_right(j)
    for i in range(SLOTS):

        @pl.when(i < count + 2)
        def _(i=i):
            each_left(jnp.int32(i), lambda copy: copy.start())

    for j in range(2, blocks):
        fetch_right(j)
    left_best[0:64, :] = before[0][...]
    left_best[64:72, :] = jnp.full((8, ROWS), -1.0, jnp.float32)
    right_best[...] = jnp.full(right_best.shape, -1.0, jnp.float32)
    pltpu.make_async_copy(right_meta, right_meta, right_sems.at[blocks]).wait()
    for k in range(blocks):
        row = right_meta[k, 0:1, : 4 * ROWS].astype(jnp.float32)
        row = jnp.where(row < 0.0, -2.0, row)
        for b in range(4):
            j = k // 4 * 4 + b
            right_tags[j : j + 1, k % 4 * ROWS : (k % 4 + 1) * ROWS] = row[:, b * ROWS : (b + 1) * ROWS]

    off_diagonal = lax.broadcasted_iota(jnp.int32, (ROWS, ROWS), 0) != lax.broadcasted_iota(jnp.int32, (ROWS, ROWS), 1)
    me = place[0]

    def arrive(i):
        each_left(i, lambda copy: copy.wait())
        j = block_of[i]
        before = block_of[jnp.maximum(i - 1, 0)]

        @pl.when((i < used[blocks + 1]) & ((i == 0) | (j != before)))
        def _():
            pltpu.make_async_copy(right_buf.at[j], right_buf.at[j], right_sems.at[j]).wait()

    def multiply(i, into):
        into[...] = lax.dot_general(
            left_buf[lax.rem(i, SLOTS)], right_buf[block_of[i]], (((1,), (1,)), ((), ())), preferred_element_type=jnp.float32
        )

    def maxima(i, scores):
        j = block_of[i]
        right_row = right_tags[pl.ds(j, 1), :]
        tops = [None] * 4
        for h in range(2):
            unit = todo[2 * i + h]
            tags = jnp.broadcast_to(left_tags[pl.ds(unit, 1), :], (ROWS, ROWS)).T
            same = (j < 4) & (unit == me * 4 + j) if columns[0] == 0 else False
            best = None
            for dy in range(4):
                cols = slice(dy * ROWS, (dy + 1) * ROWS)
                keep = tags == right_row[:, cols]
                if dy == 0 and columns[0] == 0:
                    keep = keep & (off_diagonal | jnp.logical_not(same))
                masked = jnp.where(keep, scores[h * ROWS : (h + 1) * ROWS, cols], -1.0)
                best = masked if best is None else jnp.maximum(best, masked)
                top = jnp.max(masked, axis=0, keepdims=True)
                tops[dy] = top if tops[dy] is None else jnp.maximum(tops[dy], top)
            best = jnp.max(best.T, axis=0, keepdims=True)
            left_best[pl.ds(unit, 1), :] = jnp.maximum(left_best[pl.ds(unit, 1), :], best)
        right_best[pl.ds(j, 1), :] = jnp.maximum(right_best[pl.ds(j, 1), :], jnp.concatenate(tops, axis=1))

    def refill(i):
        @pl.when(i + SLOTS < count + 2)
        def _():
            each_left(i + SLOTS, lambda copy: copy.start())

    arrive(jnp.int32(0))
    multiply(jnp.int32(0), even)

    def two(q, carry):
        i = 2 * q
        arrive(i + 1)
        multiply(i + 1, odd)
        maxima(i, even)
        refill(i)
        arrive(i + 2)
        multiply(i + 2, even)
        maxima(i + 1, odd)
        refill(i + 1)
        return carry

    lax.fori_loop(0, count // 2, two, 0)
    each_left(count + 1, lambda copy: copy.wait())
    left_out[...] = left_best[0:64, :]
    for dy in range(4):
        right_out[dy][...] = before[1 + dy][...]
        for k, dx in enumerate(columns):
            right_out[dy][dx * 4 : dx * 4 + 4, :] = right_best[k * 4 : k * 4 + 4, dy * ROWS : (dy + 1) * ROWS]


def pair_maxima(columns, steps, place, left_tags, before, left_rows, parts, metas):
    operands, known = [], {}

    def place_of(value):
        if id(value) not in known:
            known[id(value)] = len(operands)
            operands.append(value)
        return known[id(value)]

    right_at, meta_at = {}, {}
    for dx in columns:
        for dy in range(4):
            right_at[dx * 4 + dy] = [(place_of(value), base) for value, base in parts[dx, dy]]
            meta_at[dx * 4 + dy] = (place_of(metas[dx, dy][0]), metas[dx, dy][1])

    def kernel(*refs):
        pair_kernel(columns, right_at, meta_at, *refs)

    blocks = 4 * len(columns)
    smem, vmem, hbm = (pl.BlockSpec(memory_space=s) for s in (pltpu.SMEM, pltpu.VMEM, pltpu.HBM))
    return pl.pallas_call(
        kernel,
        out_shape=[jax.ShapeDtypeStruct((n, ROWS), jnp.float32) for n in (64, 16, 16, 16, 16)],
        in_specs=[smem] * 4 + [vmem] * 6 + [hbm] * (len(operands) + 1),
        out_specs=[vmem] * 5,
        scratch_shapes=[
            pltpu.VMEM((SLOTS, 2 * ROWS, 1024), jnp.bfloat16),
            pltpu.VMEM((blocks, 4 * ROWS, 1024), jnp.bfloat16),
            pltpu.VMEM((blocks, META, 1024), jnp.bfloat16),
            pltpu.VMEM((blocks, 4 * ROWS), jnp.float32),
            pltpu.VMEM((2 * ROWS, 4 * ROWS), jnp.float32),
            pltpu.VMEM((2 * ROWS, 4 * ROWS), jnp.float32),
            pltpu.VMEM((72, ROWS), jnp.float32),
            pltpu.VMEM((blocks, 4 * ROWS), jnp.float32),
            pltpu.SemaphoreType.DMA((2, 2 * SLOTS + 1)),
        ],
        compiler_params=pltpu.CompilerParams(vmem_limit_bytes=VMEM_LIMIT),
        name="pair_maxima",
    )(*steps, place, left_tags, *before, *(pltpu.with_memory_space_constraint(v, pltpu.HBM) for v in (left_rows, *operands)))


def shift(value, axis, by):
    size = lax.axis_size(axis)
    return lax.ppermute(value, axis, [((i + by) % size, i) for i in range(size)])


LINKS = {"x-": ("x", -1), "y-": ("y", -1), "x+": ("x", 1), "y+": ("y", 1)}
CARRIED = {"c": {"x+": "y+", "x-": "y-", "y+": "x-", "y-": "x+"}, "d": {"y+": "x+", "y-": "x-", "x+": "y-", "x-": "y+"}}
QUARTERS = {"x+": ("dy+", 0), "x-": ("dy-", ROWS), "y-": ("dx+", HALF1), "y+": ("dx-", HALF1 + ROWS)}
STEPS = (
    ("cx-", "cy-", "cx+", "cy+", "=", "dy-", "dy+", "bx-", "bx+"),
    ("dx-", "dx+", "by-", "by+", "ey-", "ey+", "ex-", "ex+"),
)
AFTER = {"bx": "cx", "dx": "bx", "ex": "dx", "dy": "cy", "by": "dy"}


def gather_plane(own, extra, make_beside):
    cells, cut = {}, {}

    def send(name, value):
        before = AFTER.get(name[:2])
        if before:
            other = cells[before + name[2]]
            value, other[0] = lax.optimization_barrier((value, other[0]))
        cells[name] = [shift(value, *LINKS[name[1:]])]

    for link in LINKS:
        send("a" + link, own)
    for step in STEPS[0] + STEPS[1]:
        kind, link = step[0], step[1:]
        if kind == "=":
            extra, cells["ay+"][0] = lax.optimization_barrier((extra, cells["ay+"][0]))
            for other in LINKS:
                cut[other] = cells["a" + other][0][:HALF1] if other[1] == "+" else cells["a" + other][0][HALF1:]
            cut, cells["cx+"][0], beside = lax.optimization_barrier((cut, cells["cx+"][0], make_beside(extra)))
        elif kind in CARRIED:
            send(step, cells[{"c": "a", "d": "c"}[kind] + CARRIED[kind][link]][0])
        elif kind == "b":
            send(step, cut[link])
        else:
            name, at = QUARTERS[link]
            send(step, cells[name][0][at : HALF1 if link == "x-" else at + ROWS])
    whole = {(0, 0): [own]}
    names = ("ax+", "ax-", "ay+", "ay-", "cx+", "cx-", "cy+", "cy-", "dy+", "dy-", "dx+", "dx-")
    spots = [(1, 0), (3, 0), (0, 1), (0, 3), (1, 1), (3, 3), (3, 1), (1, 3), (1, 2), (3, 2), (2, 3), (2, 1)]
    whole.update((spot, cells[name]) for spot, name in zip(spots, names))
    starts = (0, ROWS, HALF1, HALF1 + ROWS)
    parts = {key: [(v[0], at) for at in starts] for key, v in whole.items()}
    metas = {key: (v[0], 2 * ROWS) for key, v in whole.items()}
    for key, axis in (((2, 0), "x"), ((0, 2), "y")):
        h1, h2 = cells["b" + axis + "+"][0], cells["b" + axis + "-"][0]
        parts[key] = [(h1, 0), (h1, ROWS), (h2, 0), (h2, ROWS)]
        metas[key] = (h1, 2 * ROWS)
    parts[2, 2] = [(cells[name][0], 0) for name in ("ex+", "ex-", "ey-", "ey+")]
    metas[2, 2] = (cells["ex-"][0], ROWS)
    return parts, metas, beside


def pair_lists(left_lists):
    my_z, my_x, my_c = (lax.axis_index(name) for name in ("z", "x", "c"))
    place = (my_z * 2 + my_c).astype(jnp.int32).reshape(1)
    left_tags = left_lists[:, :512].astype(jnp.float32).reshape(64, ROWS)
    a, b = left_lists[:, 512:544], left_lists[:, 544:]
    group = b // BLOCKS
    mine = (group // 8 == my_z) & (group % 2 == my_c)
    dx = ((group // 2) % 4 - my_x) % 4
    unit_of = (jnp.arange(16)[:, None] * BLOCKS + a)[:, :, None]
    block = jnp.where(mine, dx * BLOCKS + b % BLOCKS, -1)
    unit_of = jnp.max(jnp.where(block[:, :, None] == jnp.arange(16), unit_of + 1, 0), axis=1).T
    left_tags = jnp.pad(left_tags, ((0, 8), (0, 0)), constant_values=-3.0)
    return [step_lists(columns, unit_of) for columns in COLUMNS], place, left_tags


def step_lists(columns, unit_of):
    blocks = 4 * len(columns)
    unit_of = jnp.concatenate([unit_of[4 * dx : 4 * dx + 4] for dx in columns])
    listed = unit_of > 0
    order = jnp.arange(16)
    rank = jnp.sum(listed[:, None, :] & (order[None, None, :] < order[None, :, None]), axis=2)
    steps = (jnp.sum(listed, axis=1) + 1) // 2
    first = jnp.sum(jnp.where(order[None, :blocks] < jnp.arange(blocks + 1)[:, None], steps[None, :], 0), axis=1)
    at = jnp.where(listed, 2 * first[:blocks, None] + rank, -1).reshape(-1)
    most = 10 * len(columns) + 4
    todo = jnp.max(jnp.where(at == jnp.arange(2 * most)[:, None], unit_of.reshape(-1), 0), axis=1)
    todo = jnp.where(todo > 0, todo - 1, 64)
    block_of = jnp.minimum(jnp.sum(first[None, 1:] <= jnp.arange(most)[:, None], axis=1), blocks - 1)
    used = jnp.concatenate([steps, (first[blocks:] + 1) // 2 * 2, first[blocks:]])
    return todo, block_of, used


def local(embeddings, cluster_ids, valid, pair_left, pair_right):
    vmem, hbm = (pl.BlockSpec(memory_space=s) for s in (pltpu.VMEM, pltpu.HBM))
    unit, full = pl.pallas_call(
        unit_kernel,
        out_shape=[jax.ShapeDtypeStruct((n, 1024), jnp.bfloat16) for n in (4 * ROWS, FULL)],
        in_specs=[vmem, vmem, hbm],
        out_specs=[vmem, vmem],
        scratch_shapes=[pltpu.VMEM(embeddings.shape, jnp.bfloat16), pltpu.SemaphoreType.DMA((BLOCKS,))],
        compiler_params=pltpu.CompilerParams(vmem_limit_bytes=VMEM_LIMIT),
        name="unit_rows",
    )(cluster_ids, valid, pltpu.with_memory_space_constraint(embeddings, pltpu.HBM))
    full, cluster_ids, pair_left = lax.optimization_barrier((full, cluster_ids, pair_left))
    left_rows = lax.all_gather(unit, ("z", "c"), axis=0, tiled=True)
    labels = jnp.where(valid > 0, cluster_ids, -1).reshape(1, -1)
    lists = jnp.concatenate([labels, (pair_left % BLOCKS)[None], pair_right[None]], axis=1)
    left_lists = lax.all_to_all(jnp.broadcast_to(lists, (16, lists.shape[1])), ("z", "c"), 0, 0, tiled=True)
    parts, metas, (steps, place, left_tags) = gather_plane(full, left_lists, pair_lists)
    found = [jnp.full((n, ROWS), -1.0, jnp.float32) for n in (64, 16, 16, 16, 16)]
    for columns, some in zip(COLUMNS, steps):
        found = pair_maxima(columns, some, place, left_tags, found, left_rows, parts, metas)
    left_best, *right_best = found
    from_left = lax.all_to_all(left_best.reshape(16, BLOCKS, ROWS), ("z", "c"), 0, 0, tiled=True)
    own = right_best[0]
    for came in [shift(right_best[dy], "y", -dy) for dy in (1, 2, 3)]:
        own = jnp.maximum(own, came)
    best = own[:BLOCKS]
    for came in [shift(own[dx * BLOCKS : (dx + 1) * BLOCKS], "x", -dx) for dx in (1, 2, 3)]:
        best = jnp.maximum(best, came)
    return jnp.maximum(jnp.max(from_left, axis=0), best)


def solution(mesh):
    wide = Mesh(mesh.devices.reshape(8, 4, 2, 4), ("z", "x", "c", "y"))
    dp = ("z", "x", "c")
    placed = (P(dp, "y", None), P(dp, "y"), P(dp, "y"), P(dp), P(dp))
    return jax.shard_map(local, mesh=wide, in_specs=placed, out_specs=P(dp, "y"), check_vma=False)
```

```python
import jax
import jax.numpy as jnp
from jax import lax
from jax.experimental import pallas as pl
from jax.experimental.pallas import tpu as pltpu
from jax.sharding import Mesh, PartitionSpec as P

epsilon = 1e-06
ROWS = 128
BLOCKS = 4
META = 16
HALF1 = 2 * ROWS + META
HALF2 = 2 * ROWS
FULL = HALF1 + HALF2
SLOTS = 8
DEPTH = 5
VMEM_LIMIT = 32 * 1024 * 1024


def unit_kernel(emb_ref, unit_ref, full_ref):
    for block in range(BLOCKS):
        rows = emb_ref[block].astype(jnp.float32)
        scale = lax.rsqrt(jnp.sum(rows * rows, axis=-1, keepdims=True) + epsilon)
        unit = (rows * scale).astype(jnp.bfloat16)
        unit_ref[block * ROWS : (block + 1) * ROWS, :] = unit
        at = block * ROWS + (META if block >= 2 else 0)
        full_ref[at : at + ROWS, :] = unit


def pair_kernel(right_at, meta_at, todo, block_of, used, place, left_tags, left_ref, *rest):
    refs = rest[:-14]
    left_out, *right_out = rest[-14:-9]
    left_buf, right_buf, right_meta, right_tags, even, odd, left_best, right_best, sems = rest[-9:]
    left_sems, right_sems = sems.at[0], sems.at[1]

    def each_right(j, act):
        for dy in range(4):
            ref, base = right_at[j // 4 * 4 + dy][j % 4]
            act(refs[ref].at[pl.ds(base, ROWS), :], right_buf.at[j, pl.ds(dy * ROWS, ROWS), :])

    def fetch_right(j):
        @pl.when(used[j] > 0)
        def _():
            each_right(j, lambda source, into: pltpu.make_async_copy(source, into, right_sems.at[j]).start())

    def each_left(i, act):
        slot = lax.rem(i, SLOTS)
        for h in range(2):
            unit = todo[2 * i + h]
            part = pl.ds(h * ROWS, ROWS)

            @pl.when(unit < 64)
            def _():
                row = pl.multiple_of(unit * ROWS, ROWS)
                act(pltpu.make_async_copy(left_ref.at[pl.ds(row, ROWS), :], left_buf.at[slot, part, :], left_sems.at[slot * 2 + h]))

    count = used[16]
    for j in range(2):
        fetch_right(j)
    for i in range(SLOTS):

        @pl.when(i < count + 2)
        def _(i=i):
            each_left(jnp.int32(i), lambda copy: copy.start())

    for k in range(16):
        ref, row = meta_at[k]
        pltpu.make_async_copy(refs[ref].at[pl.ds(row, META), :], right_meta.at[k], right_sems.at[16]).start()
    for j in range(2, 16):
        fetch_right(j)
    left_best[...] = jnp.full(left_best.shape, -1.0, jnp.float32)
    right_best[...] = jnp.full(right_best.shape, -1.0, jnp.float32)
    off_diagonal = lax.broadcasted_iota(jnp.int32, (ROWS, ROWS), 0) != lax.broadcasted_iota(jnp.int32, (ROWS, ROWS), 1)
    me = place[0]

    def arrive(i):
        each_left(i, lambda copy: copy.wait())
        j = block_of[i]
        before = block_of[jnp.maximum(i - 1, 0)]

        @pl.when((i < used[17]) & ((i == 0) | (j != before)))
        def _():
            pltpu.make_async_copy(right_buf.at[j], right_buf.at[j], right_sems.at[j]).wait()

    def multiply(i, into):
        into[...] = lax.dot_general(
            left_buf[lax.rem(i, SLOTS)], right_buf[block_of[i]], (((1,), (1,)), ((), ())), preferred_element_type=jnp.float32
        )

    def maxima(i, scores):
        j = block_of[i]
        right_row = right_tags[pl.ds(j, 1), :]
        tops = [None] * 4
        for h in range(2):
            unit = todo[2 * i + h]
            tags = jnp.broadcast_to(left_tags[pl.ds(unit, 1), :], (ROWS, ROWS)).T
            same = (j < 4) & (unit == me * 4 + j)
            best = None
            for dy in range(4):
                cols = slice(dy * ROWS, (dy + 1) * ROWS)
                keep = tags == right_row[:, cols]
                if dy == 0:
                    keep = keep & (off_diagonal | jnp.logical_not(same))
                masked = jnp.where(keep, scores[h * ROWS : (h + 1) * ROWS, cols], -1.0)
                best = masked if best is None else jnp.maximum(best, masked)
                top = jnp.max(masked, axis=0, keepdims=True)
                tops[dy] = top if tops[dy] is None else jnp.maximum(tops[dy], top)
            best = jnp.max(best.T, axis=0, keepdims=True)
            left_best[pl.ds(unit, 1), :] = jnp.maximum(left_best[pl.ds(unit, 1), :], best)
        right_best[pl.ds(j, 1), :] = jnp.maximum(right_best[pl.ds(j, 1), :], jnp.concatenate(tops, axis=1))

    def refill(i):
        @pl.when(i + SLOTS < count + 2)
        def _():
            each_left(i + SLOTS, lambda copy: copy.start())

    arrive(jnp.int32(0))
    multiply(jnp.int32(0), even)
    pltpu.make_async_copy(right_meta, right_meta, right_sems.at[16]).wait()
    for k in range(16):
        row = right_meta[k, 0:1, : 4 * ROWS].astype(jnp.float32)
        row = jnp.where(row < 0.0, -2.0, row)
        for b in range(4):
            j = k // 4 * 4 + b
            right_tags[j : j + 1, k % 4 * ROWS : (k % 4 + 1) * ROWS] = row[:, b * ROWS : (b + 1) * ROWS]

    def two(q, carry):
        i = 2 * q
        arrive(i + 1)
        multiply(i + 1, odd)
        maxima(i, even)
        refill(i)
        arrive(i + 2)
        multiply(i + 2, even)
        maxima(i + 1, odd)
        refill(i + 1)
        return carry

    lax.fori_loop(0, count // 2, two, 0)
    each_left(count + 1, lambda copy: copy.wait())
    left_out[...] = left_best[0:64, :]
    for dy in range(4):
        right_out[dy][...] = right_best[:, dy * ROWS : (dy + 1) * ROWS]


def pair_maxima(todo, block_of, used, place, left_tags, left_rows, operands, right_at, meta_at):
    def kernel(*refs):
        pair_kernel(right_at, meta_at, *refs)

    smem, vmem, hbm = (pl.BlockSpec(memory_space=s) for s in (pltpu.SMEM, pltpu.VMEM, pltpu.HBM))
    return pl.pallas_call(
        kernel,
        out_shape=[jax.ShapeDtypeStruct((n, ROWS), jnp.float32) for n in (64, 16, 16, 16, 16)],
        in_specs=[smem] * 4 + [vmem] + [hbm] * (len(operands) + 1),
        out_specs=[vmem] * 5,
        scratch_shapes=[
            pltpu.VMEM((SLOTS, 2 * ROWS, 1024), jnp.bfloat16),
            pltpu.VMEM((16, 4 * ROWS, 1024), jnp.bfloat16),
            pltpu.VMEM((16, META, 1024), jnp.bfloat16),
            pltpu.VMEM((16, 4 * ROWS), jnp.float32),
            pltpu.VMEM((2 * ROWS, 4 * ROWS), jnp.float32),
            pltpu.VMEM((2 * ROWS, 4 * ROWS), jnp.float32),
            pltpu.VMEM((72, ROWS), jnp.float32),
            pltpu.VMEM((16, 4 * ROWS), jnp.float32),
            pltpu.SemaphoreType.DMA((2, 2 * SLOTS + 1)),
        ],
        compiler_params=pltpu.CompilerParams(vmem_limit_bytes=VMEM_LIMIT),
        name="pair_maxima",
    )(todo, block_of, used, place, left_tags, *(pltpu.with_memory_space_constraint(v, pltpu.HBM) for v in (left_rows, *operands)))


def shift(value, axis, by):
    size = lax.axis_size(axis)
    return lax.ppermute(value, axis, [((i + by) % size, i) for i in range(size)])


LINKS = {"x-": ("x", -1), "y-": ("y", -1), "x+": ("x", 1), "y+": ("y", 1)}
CARRIED = {"c": {"x+": "y+", "x-": "y-", "y+": "x-", "y-": "x+"}, "d": {"y+": "x+", "y-": "x-", "x+": "y-", "x-": "y+"}}
LAST = {"x+": ("dy+", 0, ROWS), "x-": ("dy-", ROWS, HALF1 + ROWS), "y+": ("dx-", HALF1 + ROWS, FULL)}
STEPS = (
    ("cx-", "cy-", "cx+", "cy+", "=", "dy-", "dy+", "bx-", "bx+"),
    ("dx-", "dx+", "by-", "by+", "ey+", "ex-", "ex+"),
)
AFTER = {"bx": "cx", "dx": "bx", "ex": "dx", "dy": "cy", "by": "dy"}


def gather_plane(own, extra, make_beside):
    cells, cut = {}, {}

    def send(name, value):
        before = AFTER.get(name[:2])
        if before:
            other = cells[before + name[2]]
            value, other[0] = lax.optimization_barrier((value, other[0]))
        cells[name] = [shift(value, *LINKS[name[1:]])]

    for link in LINKS:
        send("a" + link, own)
    for step in STEPS[0] + STEPS[1]:
        kind, link = step[0], step[1:]
        if kind == "=":
            extra, cells["ay+"][0] = lax.optimization_barrier((extra, cells["ay+"][0]))
            for other in LINKS:
                cut[other] = cells["a" + other][0][:HALF1] if other[1] == "+" else cells["a" + other][0][HALF1:]
            cut, cells["cx+"][0], beside = lax.optimization_barrier((cut, cells["cx+"][0], make_beside(extra)))
        elif kind in CARRIED:
            send(step, cells[{"c": "a", "d": "c"}[kind] + CARRIED[kind][link]][0])
        elif kind == "b":
            send(step, cut[link])
        else:
            name, low, high = LAST[link]
            send(step, cells[name][0][low:high])
    whole = {(0, 0): [own]}
    names = ("ax+", "ax-", "ay+", "ay-", "cx+", "cx-", "cy+", "cy-", "dy+", "dy-", "dx+", "dx-")
    spots = [(1, 0), (3, 0), (0, 1), (0, 3), (1, 1), (3, 3), (3, 1), (1, 3), (1, 2), (3, 2), (2, 3), (2, 1)]
    whole.update((spot, cells[name]) for spot, name in zip(spots, names))
    starts = (0, ROWS, HALF1, HALF1 + ROWS)
    parts = {key: [(v[0], at) for at in starts] for key, v in whole.items()}
    metas = {key: (v[0], 2 * ROWS) for key, v in whole.items()}
    for key, axis in (((2, 0), "x"), ((0, 2), "y")):
        h1, h2 = cells["b" + axis + "+"][0], cells["b" + axis + "-"][0]
        parts[key] = [(h1, 0), (h1, ROWS), (h2, 0), (h2, ROWS)]
        metas[key] = (h1, 2 * ROWS)
    parts[2, 2] = [(cells["ex+"][0], 0), (cells["ex-"][0], 0), (cells["ex-"][0], ROWS + META), (cells["ey+"][0], 0)]
    metas[2, 2] = (cells["ex-"][0], ROWS)
    return parts, metas, beside


def pair_lists(left_lists):
    my_z, my_x, my_c = (lax.axis_index(name) for name in ("z", "x", "c"))
    place = (my_z * 2 + my_c).astype(jnp.int32).reshape(1)
    left_tags = left_lists[:, :512].astype(jnp.float32).reshape(64, ROWS)
    a, b = left_lists[:, 512:544], left_lists[:, 544:]
    group = b // BLOCKS
    mine = (group // 8 == my_z) & (group % 2 == my_c)
    dx = ((group // 2) % 4 - my_x) % 4
    unit_of = (jnp.arange(16)[:, None] * BLOCKS + a)[:, :, None]
    block = jnp.where(mine, dx * BLOCKS + b % BLOCKS, -1)
    unit_of = jnp.max(jnp.where(block[:, :, None] == jnp.arange(16), unit_of + 1, 0), axis=1).T.reshape(256)
    listed = (unit_of > 0).reshape(16, 16)
    order = jnp.arange(16)
    rank = jnp.sum(listed[:, None, :] & (order[None, None, :] < order[None, :, None]), axis=2)
    steps = (jnp.sum(listed, axis=1) + 1) // 2
    first = jnp.sum(jnp.where(order[None, :] < jnp.arange(17)[:, None], steps[None, :], 0), axis=1)
    at = jnp.where(listed, 2 * first[:16, None] + rank, -1).reshape(256)
    todo = jnp.max(jnp.where(at == jnp.arange(88)[:, None], unit_of, 0), axis=1)
    todo = jnp.where(todo > 0, todo - 1, 64)
    block_of = jnp.minimum(jnp.sum(first[None, 1:] <= jnp.arange(44)[:, None], axis=1), 15)
    used = jnp.concatenate([steps, (first[16:] + 1) // 2 * 2, first[16:]])
    left_tags = jnp.pad(left_tags, ((0, 8), (0, 0)), constant_values=-3.0)
    return todo, block_of, used, place, left_tags


def local(embeddings, cluster_ids, valid, pair_left, pair_right):
    limit = pltpu.CompilerParams(vmem_limit_bytes=VMEM_LIMIT)
    unit, full = pl.pallas_call(
        unit_kernel,
        out_shape=[jax.ShapeDtypeStruct((n, 1024), jnp.bfloat16) for n in (4 * ROWS, FULL)],
        compiler_params=limit,
        name="unit_rows",
    )(embeddings)
    full, cluster_ids, pair_left = lax.optimization_barrier((full, cluster_ids, pair_left))
    left_rows = lax.all_gather(unit, ("z", "c"), axis=0, tiled=True)
    labels = jnp.where(valid > 0, cluster_ids, -1).reshape(1, -1)
    lists = jnp.concatenate([labels, (pair_left % BLOCKS)[None], pair_right[None]], axis=1)
    meta = jnp.pad(labels.astype(jnp.bfloat16), ((0, META - 1), (0, 1024 - labels.shape[1])))
    full = lax.dynamic_update_slice(full, meta, (2 * ROWS, 0))
    full, lists = lax.optimization_barrier((full, lists))
    left_lists = lax.all_to_all(jnp.broadcast_to(lists, (16, lists.shape[1])), ("z", "c"), 0, 0, tiled=True)
    parts, metas, beside = gather_plane(full, left_lists, pair_lists)

    operands, known, right_at, meta_at = [], {}, [], []

    def place_of(value):
        if id(value) not in known:
            known[id(value)] = len(operands)
            operands.append(value)
        return known[id(value)]

    for k in [(dx, dy) for dx in range(4) for dy in range(4)]:
        right_at.append([(place_of(value), base) for value, base in parts[k]])
        meta_at.append((place_of(metas[k][0]), metas[k][1]))
    left_best, *right_best = pair_maxima(*beside, left_rows, operands, right_at, meta_at)
    from_left = lax.all_to_all(left_best.reshape(16, BLOCKS, ROWS), ("z", "c"), 0, 0, tiled=True)
    own = right_best[0]
    for came in [shift(right_best[dy], "y", -dy) for dy in (1, 2, 3)]:
        own = jnp.maximum(own, came)
    best = own[:BLOCKS]
    for came in [shift(own[dx * BLOCKS : (dx + 1) * BLOCKS], "x", -dx) for dx in (1, 2, 3)]:
        best = jnp.maximum(best, came)
    return jnp.maximum(jnp.max(from_left, axis=0), best)


def solution(mesh):
    wide = Mesh(mesh.devices.reshape(8, 4, 2, 4), ("z", "x", "c", "y"))
    dp = ("z", "x", "c")
    placed = (P(dp, "y", None), P(dp, "y"), P(dp, "y"), P(dp), P(dp))
    return jax.shard_map(local, mesh=wide, in_specs=placed, out_specs=P(dp, "y"), check_vma=False)
```

```python
import jax
import jax.numpy as jnp
from jax import lax
from jax.experimental import pallas as pl
from jax.experimental.pallas import tpu as pltpu
from jax.sharding import Mesh, PartitionSpec as P

epsilon = 1e-06
ROWS = 128
BLOCKS = 4
META = 16
HALF1 = 2 * ROWS + META
HALF2 = 2 * ROWS
FULL = HALF1 + HALF2
SLOTS = 8
DEPTH = 5
VMEM_LIMIT = 32 * 1024 * 1024


def unit_kernel(emb_ref, unit_ref, full_ref):
    for block in range(BLOCKS):
        rows = emb_ref[block].astype(jnp.float32)
        scale = lax.rsqrt(jnp.sum(rows * rows, axis=-1, keepdims=True) + epsilon)
        unit = (rows * scale).astype(jnp.bfloat16)
        unit_ref[block * ROWS : (block + 1) * ROWS, :] = unit
        at = block * ROWS + (META if block >= 2 else 0)
        full_ref[at : at + ROWS, :] = unit


def pair_kernel(right_at, meta_at, todo, block_of, used, place, left_tags, left_ref, *rest):
    refs = rest[:-14]
    left_out, *right_out = rest[-14:-9]
    left_buf, right_buf, right_meta, right_tags, even, odd, left_best, right_best, sems = rest[-9:]
    left_sems, right_sems = sems.at[0], sems.at[1]

    def each_right(j, act):
        for dy in range(4):
            ref, base = right_at[j // 4 * 4 + dy][j % 4]
            act(refs[ref].at[pl.ds(base, ROWS), :], right_buf.at[j, pl.ds(dy * ROWS, ROWS), :])

    def fetch_right(j):
        @pl.when(used[j] > 0)
        def _():
            each_right(j, lambda source, into: pltpu.make_async_copy(source, into, right_sems.at[j]).start())

    def each_left(i, act):
        slot = lax.rem(i, SLOTS)
        for h in range(2):
            unit = todo[2 * i + h]
            part = pl.ds(h * ROWS, ROWS)

            @pl.when(unit < 64)
            def _():
                row = pl.multiple_of(unit * ROWS, ROWS)
                act(pltpu.make_async_copy(left_ref.at[pl.ds(row, ROWS), :], left_buf.at[slot, part, :], left_sems.at[slot * 2 + h]))

    count = used[16]
    for j in range(2):
        fetch_right(j)
    for i in range(SLOTS):

        @pl.when(i < count + 2)
        def _(i=i):
            each_left(jnp.int32(i), lambda copy: copy.start())

    for k in range(16):
        ref, row = meta_at[k]
        pltpu.make_async_copy(refs[ref].at[pl.ds(row, META), :], right_meta.at[k], right_sems.at[16]).start()
    for j in range(2, 16):
        fetch_right(j)
    left_best[...] = jnp.full(left_best.shape, -1.0, jnp.float32)
    right_best[...] = jnp.full(right_best.shape, -1.0, jnp.float32)
    off_diagonal = lax.broadcasted_iota(jnp.int32, (ROWS, ROWS), 0) != lax.broadcasted_iota(jnp.int32, (ROWS, ROWS), 1)
    me = place[0]

    def arrive(i):
        each_left(i, lambda copy: copy.wait())
        j = block_of[i]
        before = block_of[jnp.maximum(i - 1, 0)]

        @pl.when((i < used[17]) & ((i == 0) | (j != before)))
        def _():
            pltpu.make_async_copy(right_buf.at[j], right_buf.at[j], right_sems.at[j]).wait()

    def multiply(i, into):
        into[...] = lax.dot_general(
            left_buf[lax.rem(i, SLOTS)], right_buf[block_of[i]], (((1,), (1,)), ((), ())), preferred_element_type=jnp.float32
        )

    def maxima(i, scores):
        j = block_of[i]
        right_row = right_tags[pl.ds(j, 1), :]
        tops = [None] * 4
        for h in range(2):
            unit = todo[2 * i + h]
            tags = jnp.broadcast_to(left_tags[pl.ds(unit, 1), :], (ROWS, ROWS)).T
            same = (j < 4) & (unit == me * 4 + j)
            best = None
            for dy in range(4):
                cols = slice(dy * ROWS, (dy + 1) * ROWS)
                keep = tags == right_row[:, cols]
                if dy == 0:
                    keep = keep & (off_diagonal | jnp.logical_not(same))
                masked = jnp.where(keep, scores[h * ROWS : (h + 1) * ROWS, cols], -1.0)
                best = masked if best is None else jnp.maximum(best, masked)
                top = jnp.max(masked, axis=0, keepdims=True)
                tops[dy] = top if tops[dy] is None else jnp.maximum(tops[dy], top)
            best = jnp.max(best.T, axis=0, keepdims=True)
            left_best[pl.ds(unit, 1), :] = jnp.maximum(left_best[pl.ds(unit, 1), :], best)
        right_best[pl.ds(j, 1), :] = jnp.maximum(right_best[pl.ds(j, 1), :], jnp.concatenate(tops, axis=1))

    def refill(i):
        @pl.when(i + SLOTS < count + 2)
        def _():
            each_left(i + SLOTS, lambda copy: copy.start())

    for i, into in ((0, even), (1, odd)):
        arrive(jnp.int32(i))
        multiply(jnp.int32(i), into)
    pltpu.make_async_copy(right_meta, right_meta, right_sems.at[16]).wait()
    for k in range(16):
        row = right_meta[k, 0:1, : 4 * ROWS].astype(jnp.float32)
        row = jnp.where(row < 0.0, -2.0, row)
        for b in range(4):
            j = k // 4 * 4 + b
            right_tags[j : j + 1, k % 4 * ROWS : (k % 4 + 1) * ROWS] = row[:, b * ROWS : (b + 1) * ROWS]

    def two(q, carry):
        i = 2 * q
        arrive(i + 2)
        arrive(i + 3)
        maxima(i, even)
        maxima(i + 1, odd)
        multiply(i + 2, even)
        multiply(i + 3, odd)
        refill(i)
        refill(i + 1)
        return carry

    lax.fori_loop(0, count // 2, two, 0)
    left_out[...] = left_best[0:64, :]
    for dy in range(4):
        right_out[dy][...] = right_best[:, dy * ROWS : (dy + 1) * ROWS]


def pair_maxima(todo, block_of, used, place, left_tags, left_rows, operands, right_at, meta_at):
    def kernel(*refs):
        pair_kernel(right_at, meta_at, *refs)

    smem, vmem, hbm = (pl.BlockSpec(memory_space=s) for s in (pltpu.SMEM, pltpu.VMEM, pltpu.HBM))
    return pl.pallas_call(
        kernel,
        out_shape=[jax.ShapeDtypeStruct((n, ROWS), jnp.float32) for n in (64, 16, 16, 16, 16)],
        in_specs=[smem] * 4 + [vmem] + [hbm] * (len(operands) + 1),
        out_specs=[vmem] * 5,
        scratch_shapes=[
            pltpu.VMEM((SLOTS, 2 * ROWS, 1024), jnp.bfloat16),
            pltpu.VMEM((16, 4 * ROWS, 1024), jnp.bfloat16),
            pltpu.VMEM((16, META, 1024), jnp.bfloat16),
            pltpu.VMEM((16, 4 * ROWS), jnp.float32),
            pltpu.VMEM((2 * ROWS, 4 * ROWS), jnp.float32),
            pltpu.VMEM((2 * ROWS, 4 * ROWS), jnp.float32),
            pltpu.VMEM((72, ROWS), jnp.float32),
            pltpu.VMEM((16, 4 * ROWS), jnp.float32),
            pltpu.SemaphoreType.DMA((2, 2 * SLOTS + 1)),
        ],
        compiler_params=pltpu.CompilerParams(vmem_limit_bytes=VMEM_LIMIT),
        name="pair_maxima",
    )(todo, block_of, used, place, left_tags, *(pltpu.with_memory_space_constraint(v, pltpu.HBM) for v in (left_rows, *operands)))


def shift(value, axis, by):
    size = lax.axis_size(axis)
    return lax.ppermute(value, axis, [((i + by) % size, i) for i in range(size)])


LINKS = {"x-": ("x", -1), "y-": ("y", -1), "x+": ("x", 1), "y+": ("y", 1)}
CARRIED = {"c": {"x+": "y+", "x-": "y-", "y+": "x-", "y-": "x+"}, "d": {"y+": "x+", "y-": "x-", "x+": "y-", "x-": "y+"}}
LAST = {"x+": ("dy+", 0, ROWS), "x-": ("dy-", ROWS, HALF1 + ROWS), "y+": ("dx-", HALF1 + ROWS, FULL)}
STEPS = (
    ("cx-", "cy-", "cx+", "cy+", "=", "dy-", "dy+", "bx-", "bx+"),
    ("dx-", "dx+", "by-", "by+", "ey+", "ex-", "ex+"),
)
AFTER = {"bx": "cx", "dx": "bx", "ex": "dx", "dy": "cy", "by": "dy"}


def gather_plane(own, extra, make_beside):
    cells, cut = {}, {}

    def send(name, value):
        before = AFTER.get(name[:2])
        if before:
            other = cells[before + name[2]]
            value, other[0] = lax.optimization_barrier((value, other[0]))
        cells[name] = [shift(value, *LINKS[name[1:]])]

    for link in LINKS:
        send("a" + link, own)
    for step in STEPS[0] + STEPS[1]:
        kind, link = step[0], step[1:]
        if kind == "=":
            extra, cells["ay+"][0] = lax.optimization_barrier((extra, cells["ay+"][0]))
            for other in LINKS:
                cut[other] = cells["a" + other][0][:HALF1] if other[1] == "+" else cells["a" + other][0][HALF1:]
            cut, cells["cx+"][0], beside = lax.optimization_barrier((cut, cells["cx+"][0], make_beside(extra)))
        elif kind in CARRIED:
            send(step, cells[{"c": "a", "d": "c"}[kind] + CARRIED[kind][link]][0])
        elif kind == "b":
            send(step, cut[link])
        else:
            name, low, high = LAST[link]
            send(step, cells[name][0][low:high])
    whole = {(0, 0): [own]}
    names = ("ax+", "ax-", "ay+", "ay-", "cx+", "cx-", "cy+", "cy-", "dy+", "dy-", "dx+", "dx-")
    spots = [(1, 0), (3, 0), (0, 1), (0, 3), (1, 1), (3, 3), (3, 1), (1, 3), (1, 2), (3, 2), (2, 3), (2, 1)]
    whole.update((spot, cells[name]) for spot, name in zip(spots, names))
    starts = (0, ROWS, HALF1, HALF1 + ROWS)
    parts = {key: [(v[0], at) for at in starts] for key, v in whole.items()}
    metas = {key: (v[0], 2 * ROWS) for key, v in whole.items()}
    for key, axis in (((2, 0), "x"), ((0, 2), "y")):
        h1, h2 = cells["b" + axis + "+"][0], cells["b" + axis + "-"][0]
        parts[key] = [(h1, 0), (h1, ROWS), (h2, 0), (h2, ROWS)]
        metas[key] = (h1, 2 * ROWS)
    parts[2, 2] = [(cells["ex+"][0], 0), (cells["ex-"][0], 0), (cells["ex-"][0], ROWS + META), (cells["ey+"][0], 0)]
    metas[2, 2] = (cells["ex-"][0], ROWS)
    return parts, metas, beside


def pair_lists(left_lists):
    my_z, my_x, my_c = (lax.axis_index(name) for name in ("z", "x", "c"))
    place = (my_z * 2 + my_c).astype(jnp.int32).reshape(1)
    left_tags = left_lists[:, :512].astype(jnp.float32).reshape(64, ROWS)
    a, b = left_lists[:, 512:544], left_lists[:, 544:]
    group = b // BLOCKS
    mine = (group // 8 == my_z) & (group % 2 == my_c)
    dx = ((group // 2) % 4 - my_x) % 4
    unit_of = (jnp.arange(16)[:, None] * BLOCKS + a)[:, :, None]
    block = jnp.where(mine, dx * BLOCKS + b % BLOCKS, -1)
    unit_of = jnp.max(jnp.where(block[:, :, None] == jnp.arange(16), unit_of + 1, 0), axis=1).T.reshape(256)
    listed = (unit_of > 0).reshape(16, 16)
    order = jnp.arange(16)
    rank = jnp.sum(listed[:, None, :] & (order[None, None, :] < order[None, :, None]), axis=2)
    steps = (jnp.sum(listed, axis=1) + 1) // 2
    first = jnp.sum(jnp.where(order[None, :] < jnp.arange(17)[:, None], steps[None, :], 0), axis=1)
    at = jnp.where(listed, 2 * first[:16, None] + rank, -1).reshape(256)
    todo = jnp.max(jnp.where(at == jnp.arange(88)[:, None], unit_of, 0), axis=1)
    todo = jnp.where(todo > 0, todo - 1, 64)
    block_of = jnp.minimum(jnp.sum(first[None, 1:] <= jnp.arange(44)[:, None], axis=1), 15)
    used = jnp.concatenate([steps, (first[16:] + 1) // 2 * 2, first[16:]])
    left_tags = jnp.pad(left_tags, ((0, 8), (0, 0)), constant_values=-3.0)
    return todo, block_of, used, place, left_tags


def local(embeddings, cluster_ids, valid, pair_left, pair_right):
    limit = pltpu.CompilerParams(vmem_limit_bytes=VMEM_LIMIT)
    unit, full = pl.pallas_call(
        unit_kernel,
        out_shape=[jax.ShapeDtypeStruct((n, 1024), jnp.bfloat16) for n in (4 * ROWS, FULL)],
        compiler_params=limit,
        name="unit_rows",
    )(embeddings)
    full, cluster_ids, pair_left = lax.optimization_barrier((full, cluster_ids, pair_left))
    left_rows = lax.all_gather(unit, ("z", "c"), axis=0, tiled=True)
    labels = jnp.where(valid > 0, cluster_ids, -1).reshape(1, -1)
    lists = jnp.concatenate([labels, (pair_left % BLOCKS)[None], pair_right[None]], axis=1)
    meta = jnp.pad(labels.astype(jnp.bfloat16), ((0, META - 1), (0, 1024 - labels.shape[1])))
    full = lax.dynamic_update_slice(full, meta, (2 * ROWS, 0))
    full, lists = lax.optimization_barrier((full, lists))
    left_lists = lax.all_to_all(jnp.broadcast_to(lists, (16, lists.shape[1])), ("z", "c"), 0, 0, tiled=True)
    parts, metas, beside = gather_plane(full, left_lists, pair_lists)

    operands, known, right_at, meta_at = [], {}, [], []

    def place_of(value):
        if id(value) not in known:
            known[id(value)] = len(operands)
            operands.append(value)
        return known[id(value)]

    for k in [(dx, dy) for dx in range(4) for dy in range(4)]:
        right_at.append([(place_of(value), base) for value, base in parts[k]])
        meta_at.append((place_of(metas[k][0]), metas[k][1]))
    left_best, *right_best = pair_maxima(*beside, left_rows, operands, right_at, meta_at)
    from_left = lax.all_to_all(left_best.reshape(16, BLOCKS, ROWS), ("z", "c"), 0, 0, tiled=True)
    own = right_best[0]
    for came in [shift(right_best[dy], "y", -dy) for dy in (1, 2, 3)]:
        own = jnp.maximum(own, came)
    best = own[:BLOCKS]
    for came in [shift(own[dx * BLOCKS : (dx + 1) * BLOCKS], "x", -dx) for dx in (1, 2, 3)]:
        best = jnp.maximum(best, came)
    return jnp.maximum(jnp.max(from_left, axis=0), best)


def solution(mesh):
    wide = Mesh(mesh.devices.reshape(8, 4, 2, 4), ("z", "x", "c", "y"))
    dp = ("z", "x", "c")
    placed = (P(dp, "y", None), P(dp, "y"), P(dp, "y"), P(dp), P(dp))
    return jax.shard_map(local, mesh=wide, in_specs=placed, out_specs=P(dp, "y"), check_vma=False)
```

```python
import jax
import jax.numpy as jnp
from jax import lax
from jax.experimental import pallas as pl
from jax.experimental.pallas import tpu as pltpu
from jax.sharding import Mesh, PartitionSpec as P

epsilon = 1e-06
ROWS = 128
BLOCKS = 4
META = 16
HALF1 = 2 * ROWS + META
HALF2 = 2 * ROWS
FULL = HALF1 + HALF2
SLOTS = 8
DEPTH = 5
VMEM_LIMIT = 32 * 1024 * 1024


def unit_kernel(emb_ref, unit_ref, full_ref):
    for block in range(BLOCKS):
        rows = emb_ref[block].astype(jnp.float32)
        scale = lax.rsqrt(jnp.sum(rows * rows, axis=-1, keepdims=True) + epsilon)
        unit = (rows * scale).astype(jnp.bfloat16)
        unit_ref[block * ROWS : (block + 1) * ROWS, :] = unit
        at = block * ROWS + (META if block >= 2 else 0)
        full_ref[at : at + ROWS, :] = unit


def pair_kernel(right_at, meta_at, todo, block_of, used, place, left_tags, left_ref, *rest):
    refs = rest[:-14]
    left_out, *right_out = rest[-14:-9]
    left_buf, right_buf, right_meta, right_tags, even, odd, left_best, right_best, sems = rest[-9:]
    left_sems, right_sems = sems.at[0], sems.at[1]

    def each_right(j, act):
        for dy in range(4):
            ref, base = right_at[j // 4 * 4 + dy][j % 4]
            act(refs[ref].at[pl.ds(base, ROWS), :], right_buf.at[j, pl.ds(dy * ROWS, ROWS), :])

    def fetch_right(j):
        @pl.when(used[j] > 0)
        def _():
            each_right(j, lambda source, into: pltpu.make_async_copy(source, into, right_sems.at[j]).start())

    def each_left(i, act):
        slot = lax.rem(i, SLOTS)
        for h in range(2):
            unit = todo[2 * i + h]
            part = pl.ds(h * ROWS, ROWS)

            @pl.when(unit < 64)
            def _():
                row = pl.multiple_of(unit * ROWS, ROWS)
                act(pltpu.make_async_copy(left_ref.at[pl.ds(row, ROWS), :], left_buf.at[slot, part, :], left_sems.at[slot * 2 + h]))

    count = used[16]
    for j in range(2):
        fetch_right(j)
    for i in range(SLOTS):

        @pl.when(i < count + 2)
        def _(i=i):
            each_left(jnp.int32(i), lambda copy: copy.start())

    for k in range(16):
        ref, row = meta_at[k]
        pltpu.make_async_copy(refs[ref].at[pl.ds(row, META), :], right_meta.at[k], right_sems.at[16]).start()
    for j in range(2, 16):
        fetch_right(j)
    left_best[...] = jnp.full(left_best.shape, -1.0, jnp.float32)
    right_best[...] = jnp.full(right_best.shape, -1.0, jnp.float32)
    off_diagonal = lax.broadcasted_iota(jnp.int32, (ROWS, ROWS), 0) != lax.broadcasted_iota(jnp.int32, (ROWS, ROWS), 1)
    me = place[0]

    def arrive(i):
        each_left(i, lambda copy: copy.wait())
        j = block_of[i]
        before = block_of[jnp.maximum(i - 1, 0)]

        @pl.when((i < used[17]) & ((i == 0) | (j != before)))
        def _():
            pltpu.make_async_copy(right_buf.at[j], right_buf.at[j], right_sems.at[j]).wait()

    def multiply(i, into):
        into[...] = lax.dot_general(
            left_buf[lax.rem(i, SLOTS)], right_buf[block_of[i]], (((1,), (1,)), ((), ())), preferred_element_type=jnp.float32
        )

    def maxima(i, scores):
        j = block_of[i]
        right_row = right_tags[pl.ds(j, 1), :]
        tops = [None] * 4
        for h in range(2):
            unit = todo[2 * i + h]
            tags = jnp.broadcast_to(left_tags[pl.ds(unit, 1), :], (ROWS, ROWS)).T
            same = (j < 4) & (unit == me * 4 + j)
            best = None
            for dy in range(4):
                cols = slice(dy * ROWS, (dy + 1) * ROWS)
                keep = tags == right_row[:, cols]
                if dy == 0:
                    keep = keep & (off_diagonal | jnp.logical_not(same))
                masked = jnp.where(keep, scores[h * ROWS : (h + 1) * ROWS, cols], -1.0)
                best = masked if best is None else jnp.maximum(best, masked)
                top = jnp.max(masked, axis=0, keepdims=True)
                tops[dy] = top if tops[dy] is None else jnp.maximum(tops[dy], top)
            best = jnp.max(best.T, axis=0, keepdims=True)
            left_best[pl.ds(unit, 1), :] = jnp.maximum(left_best[pl.ds(unit, 1), :], best)
        right_best[pl.ds(j, 1), :] = jnp.maximum(right_best[pl.ds(j, 1), :], jnp.concatenate(tops, axis=1))

    def refill(i):
        @pl.when(i + SLOTS < count + 2)
        def _():
            each_left(i + SLOTS, lambda copy: copy.start())

    for i, into in ((0, even), (1, odd)):
        arrive(jnp.int32(i))
        multiply(jnp.int32(i), into)
    pltpu.make_async_copy(right_meta, right_meta, right_sems.at[16]).wait()
    for k in range(16):
        row = right_meta[k, 0:1, : 4 * ROWS].astype(jnp.float32)
        row = jnp.where(row < 0.0, -2.0, row)
        for b in range(4):
            j = k // 4 * 4 + b
            right_tags[j : j + 1, k % 4 * ROWS : (k % 4 + 1) * ROWS] = row[:, b * ROWS : (b + 1) * ROWS]

    def two(q, carry):
        i = 2 * q
        arrive(i + 2)
        arrive(i + 3)
        maxima(i, even)
        maxima(i + 1, odd)
        multiply(i + 2, even)
        multiply(i + 3, odd)
        refill(i)
        refill(i + 1)
        return carry

    lax.fori_loop(0, count // 2, two, 0)
    left_out[...] = left_best[0:64, :]
    for dy in range(4):
        right_out[dy][...] = right_best[:, dy * ROWS : (dy + 1) * ROWS]


def pair_maxima(todo, block_of, used, place, left_tags, left_rows, operands, right_at, meta_at):
    def kernel(*refs):
        pair_kernel(right_at, meta_at, *refs)

    smem, vmem, hbm = (pl.BlockSpec(memory_space=s) for s in (pltpu.SMEM, pltpu.VMEM, pltpu.HBM))
    return pl.pallas_call(
        kernel,
        out_shape=[jax.ShapeDtypeStruct((n, ROWS), jnp.float32) for n in (64, 16, 16, 16, 16)],
        in_specs=[smem] * 4 + [vmem] + [hbm] * (len(operands) + 1),
        out_specs=[vmem] * 5,
        scratch_shapes=[
            pltpu.VMEM((SLOTS, 2 * ROWS, 1024), jnp.bfloat16),
            pltpu.VMEM((16, 4 * ROWS, 1024), jnp.bfloat16),
            pltpu.VMEM((16, META, 1024), jnp.bfloat16),
            pltpu.VMEM((16, 4 * ROWS), jnp.float32),
            pltpu.VMEM((2 * ROWS, 4 * ROWS), jnp.float32),
            pltpu.VMEM((2 * ROWS, 4 * ROWS), jnp.float32),
            pltpu.VMEM((72, ROWS), jnp.float32),
            pltpu.VMEM((16, 4 * ROWS), jnp.float32),
            pltpu.SemaphoreType.DMA((2, 2 * SLOTS + 1)),
        ],
        compiler_params=pltpu.CompilerParams(vmem_limit_bytes=VMEM_LIMIT),
        name="pair_maxima",
    )(todo, block_of, used, place, left_tags, *(pltpu.with_memory_space_constraint(v, pltpu.HBM) for v in (left_rows, *operands)))


def shift(value, axis, by):
    size = lax.axis_size(axis)
    return lax.ppermute(value, axis, [((i + by) % size, i) for i in range(size)])


LINKS = {"x-": ("x", -1), "y-": ("y", -1), "x+": ("x", 1), "y+": ("y", 1)}
CARRIED = {"c": {"x+": "y+", "x-": "y-", "y+": "x-", "y-": "x+"}, "d": {"y+": "x+", "y-": "x-", "x+": "y-", "x-": "y+"}}
LAST = {"x-": ("dy-", 0, HALF1), "y-": ("dx+", HALF1, FULL)}
STEPS = ("cx-", "cy-", "cx+", "cy+", "=", "dy-", "dx-", "dx+", "dy+", "bx+", "by+", "ex-", "ey-")
AFTER = {"bx+": "dx+", "by+": "dy+"}


def gather_plane(own, extra, make_beside):
    cells = {}

    def send(name, value):
        before = AFTER.get(name)
        if before:
            other = cells[before]
            value, other[0] = lax.optimization_barrier((value, other[0]))
        cells[name] = [shift(value, *LINKS[name[1:]])]

    for link in LINKS:
        send("a" + link, own)
    for step in STEPS:
        kind, link = step[0], step[1:]
        if kind == "=":
            extra, cells["ay+"][0] = lax.optimization_barrier((extra, cells["ay+"][0]))
            beside, cells["cx+"][0] = lax.optimization_barrier((make_beside(extra), cells["cx+"][0]))
        elif kind in CARRIED:
            send(step, cells[{"c": "a", "d": "c"}[kind] + CARRIED[kind][link]][0])
        elif kind == "b":
            send(step, cells["a" + link][0])
        else:
            name, low, high = LAST[link]
            send(step, cells[name][0][low:high])
    whole = {(0, 0): [own]}
    names = ("ax+", "ax-", "ay+", "ay-", "cx+", "cx-", "cy+", "cy-", "dy+", "dy-", "dx+", "dx-", "bx+", "by+")
    spots = [(1, 0), (3, 0), (0, 1), (0, 3), (1, 1), (3, 3), (3, 1), (1, 3), (1, 2), (3, 2), (2, 3), (2, 1), (2, 0), (0, 2)]
    whole.update((spot, cells[name]) for spot, name in zip(spots, names))
    starts = (0, ROWS, HALF1, HALF1 + ROWS)
    parts = {key: [(v[0], at) for at in starts] for key, v in whole.items()}
    metas = {key: (v[0], 2 * ROWS) for key, v in whole.items()}
    h1, h2 = cells["ex-"][0], cells["ey-"][0]
    parts[2, 2] = [(h1, 0), (h1, ROWS), (h2, 0), (h2, ROWS)]
    metas[2, 2] = (h1, 2 * ROWS)
    return parts, metas, beside


def pair_lists(left_lists):
    my_z, my_x, my_c = (lax.axis_index(name) for name in ("z", "x", "c"))
    place = (my_z * 2 + my_c).astype(jnp.int32).reshape(1)
    left_tags = left_lists[:, :512].astype(jnp.float32).reshape(64, ROWS)
    a, b = left_lists[:, 512:544], left_lists[:, 544:]
    group = b // BLOCKS
    mine = (group // 8 == my_z) & (group % 2 == my_c)
    dx = ((group // 2) % 4 - my_x) % 4
    unit_of = (jnp.arange(16)[:, None] * BLOCKS + a)[:, :, None]
    block = jnp.where(mine, dx * BLOCKS + b % BLOCKS, -1)
    unit_of = jnp.max(jnp.where(block[:, :, None] == jnp.arange(16), unit_of + 1, 0), axis=1).T.reshape(256)
    listed = (unit_of > 0).reshape(16, 16)
    order = jnp.arange(16)
    rank = jnp.sum(listed[:, None, :] & (order[None, None, :] < order[None, :, None]), axis=2)
    steps = (jnp.sum(listed, axis=1) + 1) // 2
    first = jnp.sum(jnp.where(order[None, :] < jnp.arange(17)[:, None], steps[None, :], 0), axis=1)
    at = jnp.where(listed, 2 * first[:16, None] + rank, -1).reshape(256)
    todo = jnp.max(jnp.where(at == jnp.arange(88)[:, None], unit_of, 0), axis=1)
    todo = jnp.where(todo > 0, todo - 1, 64)
    block_of = jnp.minimum(jnp.sum(first[None, 1:] <= jnp.arange(44)[:, None], axis=1), 15)
    used = jnp.concatenate([steps, (first[16:] + 1) // 2 * 2, first[16:]])
    left_tags = jnp.pad(left_tags, ((0, 8), (0, 0)), constant_values=-3.0)
    return todo, block_of, used, place, left_tags


def local(embeddings, cluster_ids, valid, pair_left, pair_right):
    limit = pltpu.CompilerParams(vmem_limit_bytes=VMEM_LIMIT)
    unit, full = pl.pallas_call(
        unit_kernel,
        out_shape=[jax.ShapeDtypeStruct((n, 1024), jnp.bfloat16) for n in (4 * ROWS, FULL)],
        compiler_params=limit,
        name="unit_rows",
    )(embeddings)
    full, cluster_ids, pair_left = lax.optimization_barrier((full, cluster_ids, pair_left))
    left_rows = lax.all_gather(unit, ("z", "c"), axis=0, tiled=True)
    labels = jnp.where(valid > 0, cluster_ids, -1).reshape(1, -1)
    lists = jnp.concatenate([labels, (pair_left % BLOCKS)[None], pair_right[None]], axis=1)
    meta = jnp.pad(labels.astype(jnp.bfloat16), ((0, META - 1), (0, 1024 - labels.shape[1])))
    full = lax.dynamic_update_slice(full, meta, (2 * ROWS, 0))
    full, lists = lax.optimization_barrier((full, lists))
    left_lists = lax.all_to_all(jnp.broadcast_to(lists, (16, lists.shape[1])), ("z", "c"), 0, 0, tiled=True)
    parts, metas, beside = gather_plane(full, left_lists, pair_lists)

    operands, known, right_at, meta_at = [], {}, [], []

    def place_of(value):
        if id(value) not in known:
            known[id(value)] = len(operands)
            operands.append(value)
        return known[id(value)]

    for k in [(dx, dy) for dx in range(4) for dy in range(4)]:
        right_at.append([(place_of(value), base) for value, base in parts[k]])
        meta_at.append((place_of(metas[k][0]), metas[k][1]))
    left_best, *right_best = pair_maxima(*beside, left_rows, operands, right_at, meta_at)
    from_left = lax.all_to_all(left_best.reshape(16, BLOCKS, ROWS), ("z", "c"), 0, 0, tiled=True)
    own = right_best[0]
    for came in [shift(right_best[dy], "y", -dy) for dy in (1, 2, 3)]:
        own = jnp.maximum(own, came)
    best = own[:BLOCKS]
    for came in [shift(own[dx * BLOCKS : (dx + 1) * BLOCKS], "x", -dx) for dx in (1, 2, 3)]:
        best = jnp.maximum(best, came)
    return jnp.maximum(jnp.max(from_left, axis=0), best)


def solution(mesh):
    wide = Mesh(mesh.devices.reshape(8, 4, 2, 4), ("z", "x", "c", "y"))
    dp = ("z", "x", "c")
    placed = (P(dp, "y", None), P(dp, "y"), P(dp, "y"), P(dp), P(dp))
    return jax.shard_map(local, mesh=wide, in_specs=placed, out_specs=P(dp, "y"), check_vma=False)
```

```python
import jax
import jax.numpy as jnp
from jax import lax
from jax.experimental import pallas as pl
from jax.experimental.pallas import tpu as pltpu
from jax.sharding import Mesh, PartitionSpec as P

epsilon = 1e-06
ROWS = 128
BLOCKS = 4
META = 16
HALF1 = 2 * ROWS + META
HALF2 = 2 * ROWS
FULL = HALF1 + HALF2
SLOTS = 12
DEPTH = 5
VMEM_LIMIT = 32 * 1024 * 1024


def unit_kernel(emb_ref, unit_ref, full_ref):
    for block in range(BLOCKS):
        rows = emb_ref[block].astype(jnp.float32)
        scale = lax.rsqrt(jnp.sum(rows * rows, axis=-1, keepdims=True) + epsilon)
        unit = (rows * scale).astype(jnp.bfloat16)
        unit_ref[block * ROWS : (block + 1) * ROWS, :] = unit
        at = block * ROWS + (META if block >= 2 else 0)
        full_ref[at : at + ROWS, :] = unit


def pair_kernel(right_at, meta_at, todo, block_of, used, place, left_tags, left_ref, *rest):
    refs = rest[:-14]
    left_out, *right_out = rest[-14:-9]
    left_buf, right_buf, right_meta, right_tags, even, odd, left_best, right_best, sems = rest[-9:]
    left_sems, right_sems = sems.at[0], sems.at[1]

    def each_right(j, act):
        for dy in range(4):
            ref, base = right_at[j // 4 * 4 + dy][j % 4]
            act(refs[ref].at[pl.ds(base, ROWS), :], right_buf.at[j, pl.ds(dy * ROWS, ROWS), :])

    def fetch_right(j):
        @pl.when(used[j] > 0)
        def _():
            each_right(j, lambda source, into: pltpu.make_async_copy(source, into, right_sems.at[j]).start())

    def each_left(i, act):
        slot = lax.rem(i, SLOTS)
        for h in range(2):
            unit = todo[2 * i + h]
            part = pl.ds(h * ROWS, ROWS)

            @pl.when(unit < 64)
            def _():
                row = pl.multiple_of(unit * ROWS, ROWS)
                act(pltpu.make_async_copy(left_ref.at[pl.ds(row, ROWS), :], left_buf.at[slot, part, :], left_sems.at[slot * 2 + h]))

    count = used[16]
    for j in range(2):
        fetch_right(j)
    for i in range(SLOTS):

        @pl.when(i < count + 2)
        def _(i=i):
            each_left(jnp.int32(i), lambda copy: copy.start())

    for k in range(16):
        ref, row = meta_at[k]
        pltpu.make_async_copy(refs[ref].at[pl.ds(row, META), :], right_meta.at[k], right_sems.at[16]).start()
    for j in range(2, 16):
        fetch_right(j)
    left_best[...] = jnp.full(left_best.shape, -1.0, jnp.float32)
    right_best[...] = jnp.full(right_best.shape, -1.0, jnp.float32)
    off_diagonal = lax.broadcasted_iota(jnp.int32, (ROWS, ROWS), 0) != lax.broadcasted_iota(jnp.int32, (ROWS, ROWS), 1)
    me = place[0]

    def arrive(i):
        each_left(i, lambda copy: copy.wait())
        j = block_of[i]
        before = block_of[jnp.maximum(i - 1, 0)]

        @pl.when((i < used[17]) & ((i == 0) | (j != before)))
        def _():
            pltpu.make_async_copy(right_buf.at[j], right_buf.at[j], right_sems.at[j]).wait()

    def multiply(i, into):
        into[...] = lax.dot_general(
            left_buf[lax.rem(i, SLOTS)], right_buf[block_of[i]], (((1,), (1,)), ((), ())), preferred_element_type=jnp.float32
        )

    def maxima(i, scores):
        j = block_of[i]
        right_row = right_tags[pl.ds(j, 1), :]
        tops = [None] * 4
        for h in range(2):
            unit = todo[2 * i + h]
            tags = jnp.broadcast_to(left_tags[pl.ds(unit, 1), :], (ROWS, ROWS)).T
            same = (j < 4) & (unit == me * 4 + j)
            best = None
            for dy in range(4):
                cols = slice(dy * ROWS, (dy + 1) * ROWS)
                keep = tags == right_row[:, cols]
                if dy == 0:
                    keep = keep & (off_diagonal | jnp.logical_not(same))
                masked = jnp.where(keep, scores[h * ROWS : (h + 1) * ROWS, cols], -1.0)
                best = masked if best is None else jnp.maximum(best, masked)
                top = jnp.max(masked, axis=0, keepdims=True)
                tops[dy] = top if tops[dy] is None else jnp.maximum(tops[dy], top)
            best = jnp.max(best.T, axis=0, keepdims=True)
            left_best[pl.ds(unit, 1), :] = jnp.maximum(left_best[pl.ds(unit, 1), :], best)
        right_best[pl.ds(j, 1), :] = jnp.maximum(right_best[pl.ds(j, 1), :], jnp.concatenate(tops, axis=1))

    def refill(i):
        @pl.when(i + SLOTS < count + 2)
        def _():
            each_left(i + SLOTS, lambda copy: copy.start())

    for i, into in ((0, even), (1, odd)):
        arrive(jnp.int32(i))
        multiply(jnp.int32(i), into)
    pltpu.make_async_copy(right_meta, right_meta, right_sems.at[16]).wait()
    for k in range(16):
        row = right_meta[k, 0:1, : 4 * ROWS].astype(jnp.float32)
        row = jnp.where(row < 0.0, -2.0, row)
        for b in range(4):
            j = k // 4 * 4 + b
            right_tags[j : j + 1, k % 4 * ROWS : (k % 4 + 1) * ROWS] = row[:, b * ROWS : (b + 1) * ROWS]

    def two(q, carry):
        i = 2 * q
        arrive(i + 2)
        arrive(i + 3)
        maxima(i, even)
        maxima(i + 1, odd)
        multiply(i + 2, even)
        multiply(i + 3, odd)
        refill(i)
        refill(i + 1)
        return carry

    lax.fori_loop(0, count // 2, two, 0)
    left_out[...] = left_best[0:64, :]
    for dy in range(4):
        right_out[dy][...] = right_best[:, dy * ROWS : (dy + 1) * ROWS]


def pair_maxima(todo, block_of, used, place, left_tags, left_rows, operands, right_at, meta_at):
    def kernel(*refs):
        pair_kernel(right_at, meta_at, *refs)

    smem, vmem, hbm = (pl.BlockSpec(memory_space=s) for s in (pltpu.SMEM, pltpu.VMEM, pltpu.HBM))
    return pl.pallas_call(
        kernel,
        out_shape=[jax.ShapeDtypeStruct((n, ROWS), jnp.float32) for n in (64, 16, 16, 16, 16)],
        in_specs=[smem] * 4 + [vmem] + [hbm] * (len(operands) + 1),
        out_specs=[vmem] * 5,
        scratch_shapes=[
            pltpu.VMEM((SLOTS, 2 * ROWS, 1024), jnp.bfloat16),
            pltpu.VMEM((16, 4 * ROWS, 1024), jnp.bfloat16),
            pltpu.VMEM((16, META, 1024), jnp.bfloat16),
            pltpu.VMEM((16, 4 * ROWS), jnp.float32),
            pltpu.VMEM((2 * ROWS, 4 * ROWS), jnp.float32),
            pltpu.VMEM((2 * ROWS, 4 * ROWS), jnp.float32),
            pltpu.VMEM((72, ROWS), jnp.float32),
            pltpu.VMEM((16, 4 * ROWS), jnp.float32),
            pltpu.SemaphoreType.DMA((2, 2 * SLOTS + 1)),
        ],
        compiler_params=pltpu.CompilerParams(vmem_limit_bytes=VMEM_LIMIT),
        name="pair_maxima",
    )(todo, block_of, used, place, left_tags, *(pltpu.with_memory_space_constraint(v, pltpu.HBM) for v in (left_rows, *operands)))


def shift(value, axis, by):
    size = lax.axis_size(axis)
    return lax.ppermute(value, axis, [((i + by) % size, i) for i in range(size)])


LINKS = {"x-": ("x", -1), "y-": ("y", -1), "x+": ("x", 1), "y+": ("y", 1)}
CARRIED = {"c": {"x+": "y+", "x-": "y-", "y+": "x-", "y-": "x+"}, "d": {"y+": "x+", "y-": "x-", "x+": "y-", "x-": "y+"}}
LAST = {"x-": ("dy-", 0, HALF1), "y-": ("dx+", HALF1, FULL)}
STEPS = ("cx-", "cy-", "cx+", "cy+", "=", "dy-", "dx-", "dx+", "dy+", "bx+", "by+", "ex-", "ey-")
AFTER = {"bx+": "dx+", "by+": "dy+"}


def gather_plane(own, extra, make_beside):
    cells = {}

    def send(name, value):
        before = AFTER.get(name)
        if before:
            other = cells[before]
            value, other[0] = lax.optimization_barrier((value, other[0]))
        cells[name] = [shift(value, *LINKS[name[1:]])]

    for link in LINKS:
        send("a" + link, own)
    for step in STEPS:
        kind, link = step[0], step[1:]
        if kind == "=":
            extra, cells["ay+"][0] = lax.optimization_barrier((extra, cells["ay+"][0]))
            beside, cells["cx+"][0] = lax.optimization_barrier((make_beside(extra), cells["cx+"][0]))
        elif kind in CARRIED:
            send(step, cells[{"c": "a", "d": "c"}[kind] + CARRIED[kind][link]][0])
        elif kind == "b":
            send(step, cells["a" + link][0])
        else:
            name, low, high = LAST[link]
            send(step, cells[name][0][low:high])
    whole = {(0, 0): [own]}
    names = ("ax+", "ax-", "ay+", "ay-", "cx+", "cx-", "cy+", "cy-", "dy+", "dy-", "dx+", "dx-", "bx+", "by+")
    spots = [(1, 0), (3, 0), (0, 1), (0, 3), (1, 1), (3, 3), (3, 1), (1, 3), (1, 2), (3, 2), (2, 3), (2, 1), (2, 0), (0, 2)]
    whole.update((spot, cells[name]) for spot, name in zip(spots, names))
    starts = (0, ROWS, HALF1, HALF1 + ROWS)
    parts = {key: [(v[0], at) for at in starts] for key, v in whole.items()}
    metas = {key: (v[0], 2 * ROWS) for key, v in whole.items()}
    h1, h2 = cells["ex-"][0], cells["ey-"][0]
    parts[2, 2] = [(h1, 0), (h1, ROWS), (h2, 0), (h2, ROWS)]
    metas[2, 2] = (h1, 2 * ROWS)
    return parts, metas, beside


def pair_lists(left_lists):
    my_z, my_x, my_c = (lax.axis_index(name) for name in ("z", "x", "c"))
    place = (my_z * 2 + my_c).astype(jnp.int32).reshape(1)
    left_tags = left_lists[:, :512].astype(jnp.float32).reshape(64, ROWS)
    a, b = left_lists[:, 512:544], left_lists[:, 544:]
    group = b // BLOCKS
    mine = (group // 8 == my_z) & (group % 2 == my_c)
    dx = ((group // 2) % 4 - my_x) % 4
    unit_of = (jnp.arange(16)[:, None] * BLOCKS + a)[:, :, None]
    block = jnp.where(mine, dx * BLOCKS + b % BLOCKS, -1)
    unit_of = jnp.max(jnp.where(block[:, :, None] == jnp.arange(16), unit_of + 1, 0), axis=1).T.reshape(256)
    listed = (unit_of > 0).reshape(16, 16)
    order = jnp.arange(16)
    rank = jnp.sum(listed[:, None, :] & (order[None, None, :] < order[None, :, None]), axis=2)
    steps = (jnp.sum(listed, axis=1) + 1) // 2
    first = jnp.sum(jnp.where(order[None, :] < jnp.arange(17)[:, None], steps[None, :], 0), axis=1)
    at = jnp.where(listed, 2 * first[:16, None] + rank, -1).reshape(256)
    todo = jnp.max(jnp.where(at == jnp.arange(88)[:, None], unit_of, 0), axis=1)
    todo = jnp.where(todo > 0, todo - 1, 64)
    block_of = jnp.minimum(jnp.sum(first[None, 1:] <= jnp.arange(44)[:, None], axis=1), 15)
    used = jnp.concatenate([steps, (first[16:] + 1) // 2 * 2, first[16:]])
    left_tags = jnp.pad(left_tags, ((0, 8), (0, 0)), constant_values=-3.0)
    return todo, block_of, used, place, left_tags


def local(embeddings, cluster_ids, valid, pair_left, pair_right):
    limit = pltpu.CompilerParams(vmem_limit_bytes=VMEM_LIMIT)
    unit, full = pl.pallas_call(
        unit_kernel,
        out_shape=[jax.ShapeDtypeStruct((n, 1024), jnp.bfloat16) for n in (4 * ROWS, FULL)],
        compiler_params=limit,
        name="unit_rows",
    )(embeddings)
    full, cluster_ids, pair_left = lax.optimization_barrier((full, cluster_ids, pair_left))
    left_rows = lax.all_gather(unit, ("z", "c"), axis=0, tiled=True)
    labels = jnp.where(valid > 0, cluster_ids, -1).reshape(1, -1)
    lists = jnp.concatenate([labels, (pair_left % BLOCKS)[None], pair_right[None]], axis=1)
    meta = jnp.pad(labels.astype(jnp.bfloat16), ((0, META - 1), (0, 1024 - labels.shape[1])))
    full = lax.dynamic_update_slice(full, meta, (2 * ROWS, 0))
    full, lists = lax.optimization_barrier((full, lists))
    left_lists = lax.all_to_all(jnp.broadcast_to(lists, (16, lists.shape[1])), ("z", "c"), 0, 0, tiled=True)
    parts, metas, beside = gather_plane(full, left_lists, pair_lists)

    operands, known, right_at, meta_at = [], {}, [], []

    def place_of(value):
        if id(value) not in known:
            known[id(value)] = len(operands)
            operands.append(value)
        return known[id(value)]

    for k in [(dx, dy) for dx in range(4) for dy in range(4)]:
        right_at.append([(place_of(value), base) for value, base in parts[k]])
        meta_at.append((place_of(metas[k][0]), metas[k][1]))
    left_best, *right_best = pair_maxima(*beside, left_rows, operands, right_at, meta_at)
    from_left = lax.all_to_all(left_best.reshape(16, BLOCKS, ROWS), ("z", "c"), 0, 0, tiled=True)
    own = right_best[0]
    for came in [shift(right_best[dy], "y", -dy) for dy in (1, 2, 3)]:
        own = jnp.maximum(own, came)
    best = own[:BLOCKS]
    for came in [shift(own[dx * BLOCKS : (dx + 1) * BLOCKS], "x", -dx) for dx in (1, 2, 3)]:
        best = jnp.maximum(best, came)
    return jnp.maximum(jnp.max(from_left, axis=0), best)


def solution(mesh):
    wide = Mesh(mesh.devices.reshape(8, 4, 2, 4), ("z", "x", "c", "y"))
    dp = ("z", "x", "c")
    placed = (P(dp, "y", None), P(dp, "y"), P(dp, "y"), P(dp), P(dp))
    return jax.shard_map(local, mesh=wide, in_specs=placed, out_specs=P(dp, "y"), check_vma=False)
```
